128 devices in a mesh: dp: 8 (over x, y_hi), ctx: 8 (over z, core), tensor: 2 (over y_lo).
Axes of the slice: x: 4, y: 4 (y_hi: 2, y_lo: 2; y = y_hi * 2 + y_lo), z: 4, core: 2. Of those that a mesh axis runs over, the one named last changes fastest.
Arguments:
- activations: bfloat16 [8192, 1024], P(('dp', 'ctx')), may hold values from -6 to 6
- cotangent: bfloat16 [8192, 1024], P(('dp', 'ctx')), may hold values from -6 to 6
- segment_ids: int32 [8, 1024], P('dp'), may hold values from 0 to 4, as said below
- expert_ids: int32 [1, 8192, 8], P(None, 'dp'), may hold values from 0 to 31, all different within a row; in each aligned block of 128 rows (0 to 127, 128 to 255, ..., all dimensions but the last counted through in order) at most 40 rows name the same one
- gate_weights: float32 [1, 8192, 8], P(None, 'dp'), may hold values from 0.06 to 0.25
- norm_gains: bfloat16 [1, 2, 1024], P(None, None, 'dp'), may hold values from 0.5 to 1.5
- w_query: bfloat16 [1, 1024, 1024], P(None, 'dp'), may hold values from -0.1875 to 0.1875
- w_keyval: bfloat16 [1, 1024, 1024], P(None, 'dp'), may hold values from -0.1875 to 0.1875
- w_out: bfloat16 [1, 1024, 1024], P(None, 'dp'), may hold values from -1.5 to 1.5
- w_gateup: bfloat16 [1, 32, 1024, 2, 512], P(None, 'ctx', 'dp', None, 'tensor'), may hold values from -0.1875 to 0.1875
- w_down: bfloat16 [1, 32, 512, 1024], P(None, 'ctx', 'tensor', 'dp'), may hold values from -1 to 1
Outputs:
- activations_out: bfloat16 [8192, 1024], P(('dp', 'ctx'))
- grad_activations: float32 [8192, 1024], P(('dp', 'ctx'))
- grad_gains: float32 [1, 2, 1024], P(None, None, ('dp', 'ctx'))
- grad_query: float32 [1, 1024, 1024], P(None, ('dp', 'ctx'))
- grad_keyval: float32 [1, 1024, 1024], P(None, ('dp', 'ctx'))
- grad_out: float32 [1, 1024, 1024], P(None, ('dp', 'ctx'))
- grad_gateup: float32 [1, 32, 1024, 2, 512], P(None, 'ctx', 'dp', None, 'tensor')
- grad_down: float32 [1, 32, 512, 1024], P(None, 'ctx', 'tensor', 'dp')
The draws below stay inside these ranges and needn't reach their ends.
Inputs may be any that keep to these rules, and one draw needn't show every extreme that they name: `segment_ids`: along a row the numbers never fall; one document of every row begins within the first 32 positions and ends within the last 32. `expert_ids`: the 8 experts of a token differ; in the rows of one device of one layer (aligned blocks of 128 rows) no expert is named more than 40 times.
All inputs are finite; a program needn't handle non-finite values.
Results may differ from the reference program's by a relative error of at most 0.015.
Values may be sent and summed in bfloat16 or wider, within the bound.
A program may use at most 128 MiB of HBM per device.

```python
import math
import jax
import jax.numpy as jnp
import numpy as np
from jax import lax

D = 1024
HQ = 16
KVH = 8
HD = 64
F = 512
EXPERTS = 32
TOP = 8
LAYERS = 1
PACKED = 1024
ROWS = 128
TOKENS = 8192
N_DP = 8


def draw_segment_ids(key, part):
    key = jax.random.fold_in(key, 11)
    quarter = ROWS // 4
    first_key, second_key, third_key = jax.random.split(key, 3)
    leading = jax.random.randint(first_key, (N_DP, 1), 1, quarter)
    first_cut = jax.random.randint(second_key, (N_DP, 1), 1, leading + 1)
    tail_start = leading + PACKED - quarter
    last_cut = jax.random.randint(third_key, (N_DP, 1), tail_start, PACKED)
    places = jnp.arange(PACKED, dtype=jnp.int32)[None, :]
    total = (places >= first_cut).astype(jnp.int32) + (places >= leading).astype(jnp.int32)
    total = total + (places >= tail_start).astype(jnp.int32) + (places >= last_cut).astype(jnp.int32)
    return total.astype(jnp.int32)


def shard_levels(stream_key, extent, shards, smallest, top_value):
    loudness = 1.0
    for dim, parts in shards:
        steps = jax.random.uniform(jax.random.fold_in(jax.random.fold_in(stream_key, 6), dim), (parts,), jnp.float32, smallest / len(shards), top_value / len(shards))
        loudness = loudness * jnp.repeat(jnp.exp(steps), extent[dim] // parts).reshape((-1,) + (1,) * (len(extent) - 1 - dim))
    return loudness


def assign_block(rng, own, number, rows, number_of, top, limit, slope):
    ranking = jax.random.permutation(rng, number_of)
    crowded, ordinary = portions_of(number_of, rows * top, limit, slope, True), portions_of(number_of, rows * top, limit, slope, False)
    places = jnp.arange(number_of)

    def named(lengths, turn):
        used = int((lengths > 0).sum())
        fixed = max(1, used // 4)
        passed = fixed + (places - fixed + turn * (used - fixed)) % max(1, number_of - fixed)
        return jnp.zeros((number_of,), jnp.int32).at[ranking[jnp.where(places < fixed, places, passed)]].set(jnp.asarray(lengths, jnp.int32))

    lengths = jnp.where(number % 4 == 0, named(crowded, number // 4), named(ordinary, number - number // 4 - 1))
    mixed = jax.random.permutation(jax.random.fold_in(own, 3), number_of)
    giver, taker = mixed[0:number_of // 2 * 2:2], mixed[1:number_of // 2 * 2:2]
    slack = jnp.minimum(lengths[giver] - 1, limit - lengths[taker]) // 2
    slack = jnp.where((giver == ranking[0]) | (taker == ranking[0]) | (lengths[taker] == 0), 0, jnp.maximum(slack, 0))
    passed = jax.random.randint(jax.random.fold_in(own, 4), (number_of // 2,), 0, 1 << 20) % (slack + 1)
    lengths = lengths.at[giver].add(-passed).at[taker].add(passed)
    members = jnp.searchsorted(jnp.cumsum(lengths), jnp.arange(rows * top), side="right").astype(jnp.int32)
    table = members.reshape(top, rows).T
    table = table[jax.random.permutation(jax.random.fold_in(own, 1), rows)]
    turn = jax.random.randint(jax.random.fold_in(own, 2), (rows, 1), 0, top)
    return jnp.take_along_axis(table, (jnp.arange(top)[None, :] + turn) % top, axis=1)


def portions_of(amount, total, most, skew, full):
    weights = [(1 << 20) // math.isqrt(rank ** skew) + 1 for rank in range(1, amount + 1)]
    largest = most if full else min(most, max(-(-total // amount), total * weights[0] // sum(weights)))
    least = 1 if total - largest >= amount - 1 else 0
    given, surplus = [largest] + [least] * (amount - 1), total - largest - least * (amount - 1)
    while surplus > 0:
        candidates = [i for i in range(1, amount) if given[i] < largest] or [i for i in range(1, amount) if given[i] < most]
        whole, budget = sum([weights[i] for i in candidates]), surplus
        for i in candidates:
            addition = min(most - given[i], max(1, budget * weights[i] // whole), surplus)
            given[i] = given[i] + addition
            surplus = surplus - addition
    return np.array(given)


def centred(own_key, shape, deviation, bound, cuts=(), kind=jnp.bfloat16):
    factor_of = shard_levels(own_key, shape, cuts, -0.22, 0.18) if cuts else 1.0
    values = jax.random.normal(own_key, shape, jnp.float32) * deviation * factor_of
    return jnp.minimum(jnp.maximum(values, -bound), bound).astype(kind)


def setup_inputs(seed: int = 0) -> dict:
    keys = jax.random.split(jax.random.key(seed), 12)
    activations = centred(keys[0], (TOKENS, D), 1.0, 6.0, ((0, 64),))
    cotangent = centred(keys[1], (TOKENS, D), 1.0, 6.0, ((0, 64),))
    segment_ids = draw_segment_ids(jax.random.fold_in(keys[11], 71), 0)
    expert_ids_keys = jax.random.split(jax.random.fold_in(keys[3], 1), LAYERS * TOKENS // ROWS)
    expert_ids_turns = jax.random.permutation(jax.random.fold_in(keys[3], 3), LAYERS * TOKENS // ROWS)
    expert_ids = jax.vmap(lambda own, number: assign_block(jax.random.fold_in(keys[3], 2), own, number, ROWS, EXPERTS, TOP, ROWS * 5 // 16, 1))(expert_ids_keys, expert_ids_turns).reshape((LAYERS, TOKENS, TOP))
    gate_weights = jnp.clip(jnp.exp(math.log(0.25) - 1.4271164 * jax.random.uniform(keys[4], (LAYERS, TOKENS, TOP), jnp.float32) ** shard_levels(keys[4], (LAYERS, TOKENS, TOP), ((1, 8),), -0.2, 0.2)), 0.06, 0.25)
    norm_gains = jnp.clip(1.0 + 0.1 * jax.random.normal(keys[5], (LAYERS, 2, D), jnp.float32), 0.5, 1.5).astype(jnp.bfloat16)
    w_query = centred(keys[6], (LAYERS, D, HQ * HD), D ** -0.5, 0.1875, ((1, 8),))
    w_keyval = centred(keys[7], (LAYERS, D, 2 * KVH * HD), D ** -0.5, 0.1875, ((1, 8),))
    w_out = centred(keys[8], (LAYERS, HQ * HD, D), (HQ * HD // 64) ** -0.5, 1.5, ((1, 8),))
    w_gateup = centred(keys[9], (LAYERS, EXPERTS, D, 2, F), D ** -0.5, 0.1875, ((1, 8), (2, 8), (4, 2)))
    w_down = centred(keys[10], (LAYERS, EXPERTS, F, D), (F // 16) ** -0.5, 1.0, ((1, 8), (2, 2), (3, 8)))
    return {"activations": activations, "cotangent": cotangent, "segment_ids": segment_ids, "expert_ids": expert_ids, "gate_weights": gate_weights, "norm_gains": norm_gains, "w_query": w_query, "w_keyval": w_keyval, "w_out": w_out, "w_gateup": w_gateup, "w_down": w_down}


EPSILON = 1e-06
NEGATIVE = -1e+30
HIGHEST = lax.Precision.HIGHEST

@jax.custom_vjp
def low(v):
    return lax.optimization_barrier(v.astype(jnp.bfloat16)).astype(jnp.float32)

@jax.custom_vjp
def low_back(v):
    return v

def low_keep(v):
    return (low(v), None)

def low_pass(kept, grad):
    return (grad,)

def back_keep(v):
    return (v, None)

def back_low(kept, grad):
    return (low(grad),)
low.defvjp(low_keep, low_pass)
low_back.defvjp(back_keep, back_low)

def rms_norm(values, gain):
    return values * lax.rsqrt(lax.optimization_barrier(jnp.mean(values * values, axis=-1, keepdims=True)) + EPSILON) * gain

def rope_tables(segment):
    length = segment.shape[0]
    places = jnp.arange(length, dtype=jnp.int32)
    starts = jnp.concatenate([jnp.ones((1,), dtype=bool), segment[1:] != segment[:-1]])
    first_place = lax.cummax(jnp.where(starts, places, 0), axis=0)
    offsets = (places - first_place).astype(jnp.float32)
    frequency = jnp.exp(jnp.arange(HD // 2, dtype=jnp.float32) * (-2.0 * math.log(10000.0) / HD))
    angles = offsets[:, None] * frequency[None, :]
    return (jnp.cos(angles), jnp.sin(angles))

def rotate(values, cosine, sine):
    half_width = values.shape[-1] // 2
    first_half = values[..., :half_width]
    second_half = values[..., half_width:]
    return jnp.concatenate([first_half * cosine - second_half * sine, second_half * cosine + first_half * sine], axis=-1)

def block_forward(params, residual, segment, route_ids, route_gates):
    norm_gains, w_query, w_keyval, w_out, w_gateup, w_down = params
    cosine, sine = rope_tables(segment)
    places = jnp.arange(PACKED, dtype=jnp.int32)
    allowed = (segment[:, None] == segment[None, :]) & (places[:, None] >= places[None, :])
    expert_list = jnp.arange(EXPERTS, dtype=jnp.int32)
    scale = 1.0 / math.sqrt(HD)
    for layer_index in range(LAYERS):
        normed = low(rms_norm(residual, norm_gains[layer_index, 0]))
        query = jnp.dot(normed, w_query[layer_index], precision=HIGHEST).reshape(PACKED, KVH, 2, HD)
        keyval = jnp.dot(normed, w_keyval[layer_index], precision=HIGHEST).reshape(PACKED, KVH, 2, HD)
        query = low(rotate(low_back(query), cosine[:, None, None, :], sine[:, None, None, :]))
        key_rows = low(rotate(low_back(keyval[:, :, 0]), cosine[:, None, :], sine[:, None, :]))
        value_rows = low(low_back(keyval[:, :, 1]))

        def one_head(inputs):
            head_query, head_key, head_value = inputs
            scores = jnp.einsum('qgd,kd->gqk', head_query, head_key, precision=HIGHEST) * scale
            scores = low_back(scores)
            scores = jnp.where(allowed[None], scores, NEGATIVE)
            largest = lax.optimization_barrier(jnp.max(scores, axis=-1, keepdims=True))
            expon = jnp.exp(scores - largest)
            probs = expon / lax.optimization_barrier(jnp.sum(expon, axis=-1, keepdims=True))
            return jnp.einsum('gqk,kd->qgd', low(probs), head_value, precision=HIGHEST)
        attended = lax.map(jax.checkpoint(one_head), (query.transpose(1, 0, 2, 3), key_rows.transpose(1, 0, 2), value_rows.transpose(1, 0, 2)))
        attended = low(low_back(attended.transpose(1, 0, 2, 3).reshape(PACKED, HQ * HD)))
        residual = residual + low_back(jnp.dot(attended, w_out[layer_index], precision=HIGHEST))
        normed_two = low(rms_norm(residual, norm_gains[layer_index, 1]))
        share = lax.optimization_barrier(jnp.sum(route_gates[layer_index][:, :, None] * (route_ids[layer_index][:, :, None] == expert_list).astype(jnp.float32), axis=1))

        def one_expert(total, inputs):
            gateup_weight, down_weight, weight = inputs
            gate_up = low_back(jnp.einsum('td,djf->tjf', normed_two, gateup_weight, precision=HIGHEST))
            hidden = low(jax.nn.silu(gate_up[:, 0]) * gate_up[:, 1])
            output = low_back(jnp.dot(hidden, down_weight, precision=HIGHEST))
            return (total + weight[:, None] * output, None)
        mixture, unused = lax.scan(jax.checkpoint(one_expert), jnp.zeros_like(residual), (w_gateup[layer_index], w_down[layer_index], share.T))
        residual = residual + low_back(mixture)
    return residual

def reference(activations, cotangent, segment_ids, expert_ids, gate_weights, norm_gains, w_query, w_keyval, w_out, w_gateup, w_down):
    params = (norm_gains.astype(jnp.float32), w_query.astype(jnp.float32), w_keyval.astype(jnp.float32), w_out.astype(jnp.float32), w_gateup.astype(jnp.float32), w_down.astype(jnp.float32))
    inputs = activations.astype(jnp.float32).reshape(N_DP, PACKED, D)
    route_ids = expert_ids.reshape(LAYERS, N_DP, PACKED, TOP).transpose(1, 0, 2, 3)
    route_gates = gate_weights.astype(jnp.float32).reshape(LAYERS, N_DP, PACKED, TOP).transpose(1, 0, 2, 3)

    def forward(weights, rows_in):

        def one_row(inputs_row):
            row_values, row_segment, row_ids, row_gates = inputs_row
            return block_forward(weights, row_values, row_segment, row_ids, row_gates)
        return lax.map(jax.checkpoint(one_row), (rows_in, segment_ids, route_ids, route_gates))
    outputs, pullback = jax.vjp(forward, params, inputs)
    grads, grad_inputs = pullback(cotangent.astype(jnp.float32).reshape(N_DP, PACKED, D))
    return (outputs.reshape(TOKENS, D).astype(jnp.bfloat16), grad_inputs.reshape(TOKENS, D), grads[0], grads[1], grads[2], grads[3], grads[4], grads[5])
```

```python
import math

import jax
import jax.numpy as jnp
import numpy as np
from jax import lax
from jax.experimental import pallas as pl
from jax.experimental.pallas import tpu as pltpu
from jax.sharding import PartitionSpec as P

D = 1024
HD = 64
T = 1024
ROWS = 128
N_DP = 8
N_CTX = 8
LOCAL_EXPERTS = 4
CAP = 40
PAIRS = 4
SLOTS = 2 * CAP
FH = 256
BLOCK = 256
EPSILON = 1e-06
NEGATIVE = -1e30
SCALE = 1.0 / math.sqrt(HD)
BF16 = jnp.bfloat16
F32 = jnp.float32
VMEM_LIMIT = 62 * 1024 * 1024
WIDE = 2 * FH + 256
LATE = 2
SOON = LOCAL_EXPERTS - LATE
COPIES = 224


def dot(a, b, dims=((1,), (0,))):
    return lax.dot_general(a, b, (dims, ((), ())), preferred_element_type=F32)


def rms_norm(values, gain):
    return values * lax.rsqrt(jnp.mean(values * values, axis=-1, keepdims=True) + EPSILON) * gain


def swap_halves(values):
    lane = lax.broadcasted_iota(jnp.int32, values.shape, 1)
    return jnp.where(lane % HD < HD // 2, pltpu.roll(values, 96, 1), pltpu.roll(values, 32, 1))


def low_lanes(shape):
    return lax.broadcasted_iota(jnp.int32, shape, 1) < HD


class Links:
    def __init__(self, send, recv):
        self.send, self.recv, self.made, self.settled = send, recv, [], []

    def copy(self, src, dst, **device):
        place = len(self.made)
        assert place < COPIES
        made = pltpu.make_async_remote_copy(
            src_ref=src,
            dst_ref=dst,
            send_sem=self.send.at[place],
            recv_sem=self.recv.at[place],
            device_id=device,
            device_id_type=pl.DeviceIdType.MESH,
        )
        self.made.append(made)
        return made

    def start(self, src, dst, **device):
        made = self.copy(src, dst, **device)
        made.start()
        return made

    def settle(self, copies):
        for made in copies:
            made.wait_send()
            self.settled.append(id(made))

    def finish(self, skip=()):
        for made in self.made:
            if id(made) not in self.settled and not any(made is each for each in skip):
                made.wait_send()


def ctx_places():
    me = lax.axis_index("ctx")
    z, core = me // 2, me % 2
    at = lambda step: lax.rem(z + step, 4) * 2 + core
    return me, z * 2 + 1 - core, at(1), at(3), at(2)


def dp_places():
    me = lax.axis_index("dp")
    x, high = me // 2, me % 2
    at = lambda step: lax.rem(x + step, 4)
    return x, high, at(1), at(3), at(2)


class RowGather:
    def __init__(self, links, full):
        self.links, self.full = links, full
        self.me, self.sib, self.up, self.down, self.far = ctx_places()

    def start(self, own):
        full, mine = self.full, self.full.at[self.me]
        half = full.shape[1] // 2
        first, rest = pl.ds(0, half), pl.ds(half, half)
        self.to_up = self.links.start(own.at[first], mine.at[first], ctx=self.up)
        self.to_down = self.links.start(own.at[rest], mine.at[rest], ctx=self.down)
        self.rest_up = self.links.start(own.at[rest], mine.at[rest], ctx=self.up)
        self.rest_down = self.links.start(own.at[first], mine.at[first], ctx=self.down)
        self.to_sib = [self.links.start(own, mine, ctx=self.sib)]

    def pass_on(self):
        full, links = self.full, self.links
        half = full.shape[1] // 2
        self.to_up.wait_recv()
        part = full.at[self.down, pl.ds(0, half)]
        self.far_up = links.start(part, part, ctx=self.up)
        self.to_down.wait_recv()
        part = full.at[self.up, pl.ds(half, half)]
        self.far_down = links.start(part, part, ctx=self.down)
        for place, arrival in ((self.down, self.rest_up), (self.up, self.rest_down)):
            arrival.wait_recv()
            part = full.at[place]
            self.to_sib.append(links.start(part, part, ctx=self.sib))

    def pass_far(self):
        full, links = self.full, self.links
        half = full.shape[1] // 2
        for arrival, first in ((self.far_up, 0), (self.far_down, half)):
            arrival.wait_recv()
            part = full.at[self.far, pl.ds(first, half)]
            self.to_sib.append(links.start(part, part, ctx=self.sib))

    def all(self):
        return [self.to_up, self.to_down, self.rest_up, self.rest_down, self.far_up, self.far_down] + self.to_sib

    def finish(self):
        for made in self.to_sib:
            made.wait_recv()


class RowSum:
    def __init__(self, links, part, near, mid, last):
        self.links, self.part, self.near, self.mid, self.last = links, part, near, mid, last
        self.me, self.sib, self.up, self.down, self.far = ctx_places()
        self.core = self.me % 2
        self.sent = []

    def send(self, z):
        self.sent.append(self.links.start(self.part.at[2 * z + 1 - self.core], self.near.at[z], ctx=self.sib))

    def add(self, place):
        z = place // 2
        self.near[z] = (self.near[z].astype(F32) + self.part[2 * z + self.core].astype(F32)).astype(BF16)

    def pair(self):
        links, near, half = self.links, self.near, self.near.shape[1] // 2
        for made in self.sent:
            made.wait_recv()
        self.add(self.far)
        far = self.far // 2
        self.far_up = links.start(near.at[far, pl.ds(0, half)], self.mid.at[0], ctx=self.up)
        self.far_down = links.start(near.at[far, pl.ds(half, half)], self.mid.at[1], ctx=self.down)
        up, down = self.up // 2, self.down // 2
        self.add(self.up)
        self.rest_up = links.start(near.at[up, pl.ds(half, half)], self.last.at[0, pl.ds(half, half)], ctx=self.up)
        self.add(self.down)
        self.rest_down = links.start(near.at[down, pl.ds(0, half)], self.last.at[1, pl.ds(0, half)], ctx=self.down)
        self.add(self.me)

    def pass_on(self):
        links, near, half = self.links, self.near, self.near.shape[1] // 2
        up, down = self.up // 2, self.down // 2
        self.far_up.wait_recv()
        near[up, 0:half] = (near[up, 0:half].astype(F32) + self.mid[0].astype(F32)).astype(BF16)
        self.to_up = links.start(near.at[up, pl.ds(0, half)], self.last.at[0, pl.ds(0, half)], ctx=self.up)
        self.far_down.wait_recv()
        near[down, half:] = (near[down, half:].astype(F32) + self.mid[1].astype(F32)).astype(BF16)
        self.to_down = links.start(
            near.at[down, pl.ds(half, half)], self.last.at[1, pl.ds(half, half)], ctx=self.down
        )

    def finish(self):
        for made in (self.rest_up, self.rest_down, self.to_up, self.to_down):
            made.wait_recv()
        return self.near[self.me // 2].astype(F32) + (self.last[0].astype(F32) + self.last[1].astype(F32))


def greet():
    barrier = pltpu.get_barrier_semaphore()
    dp, ctx = lax.axis_index("dp"), lax.axis_index("ctx")

    def signal(**device):
        pl.semaphore_signal(barrier, inc=1, device_id=device, device_id_type=pl.DeviceIdType.MESH)

    for step in range(1, 8):
        signal(ctx=lax.rem(ctx + step, 8))
        signal(dp=lax.rem(dp + step, 8))
    signal(tensor=1 - lax.axis_index("tensor"))
    signal(dp=dp + 1 - 2 * lax.rem(dp, 2), tensor=1 - lax.axis_index("tensor"))

    @pl.when(dp != ctx)
    def _():
        signal(dp=ctx, ctx=dp)
        pl.semaphore_wait(barrier, 17)

    @pl.when(dp == ctx)
    def _():
        pl.semaphore_wait(barrier, 16)


def y_places():
    dp, tensor = lax.axis_index("dp"), lax.axis_index("tensor")
    same, other = dp, dp + 1 - 2 * lax.rem(dp, 2)
    up = jnp.where(tensor == 0, same, other)
    return up, same + other - up, 1 - tensor


class Across:
    def __init__(self, links, relay, target):
        self.links, self.relay, self.target = links, relay, target
        self.up, self.down, self.tensor = y_places()

    def start(self, halves):
        self.first = [
            self.links.start(halves[0], self.relay.at[0], dp=self.up, tensor=self.tensor),
            self.links.start(halves[1], self.relay.at[1], dp=self.down, tensor=self.tensor),
        ]

    def pass_on(self):
        self.second = []
        for way, to in ((0, self.up), (1, self.down)):
            self.first[way].wait_recv()
            self.second.append(
                self.links.start(self.relay.at[way], self.target(way, to), dp=to, tensor=self.tensor)
            )

    def finish(self):
        for made in self.second:
            made.wait_recv()


class WeightGather:
    def __init__(self, links, full, relay, expert, late):
        self.links, self.full, self.expert, self.late = links, full, expert, late
        self.x, self.high, self.up, self.down, self.far = dp_places()
        if late:
            target = lambda way, to: full.at[:, 1 - lax.rem(to, 2), expert, pl.ds(64 * way, 64)]
        else:
            target = lambda way, to: full.at[self.x, 1 - lax.rem(to, 2), expert, pl.ds(64 * way, 64)]
        self.across = Across(links, relay, target)

    def both(self, src, dst):
        return (
            self.links.start(src, dst, dp=self.up * 2 + self.high),
            self.links.start(src, dst, dp=self.down * 2 + self.high),
        )

    def start(self, own):
        self.own = self.both(own, self.full.at[self.x, self.high, self.expert])
        if not self.late:
            self.across.start([own.at[pl.ds(64 * way, 64)] for way in range(2)])

    def relay(self, arrivals, high):
        arrivals[0].wait_recv()
        part = self.full.at[self.down, high, self.expert, pl.ds(0, 64)]
        first = self.links.start(part, part, dp=self.up * 2 + self.high)
        arrivals[1].wait_recv()
        part = self.full.at[self.up, high, self.expert, pl.ds(64, 64)]
        return first, self.links.start(part, part, dp=self.down * 2 + self.high)

    def pass_own(self):
        self.far_own = self.relay(self.own, self.high)

    def y_start(self):
        for made in self.far_own:
            made.wait_recv()
        self.across.start(
            [self.full.at[:, self.high, self.expert, pl.ds(64 * way, 64)] for way in range(2)]
        )

    def y_pass(self):
        self.across.pass_on()

    def pass_other(self):
        self.across.finish()
        part = self.full.at[self.x, 1 - self.high, self.expert]
        self.other = self.both(part, part)

    def pass_last(self):
        self.far_other = self.relay(self.other, 1 - self.high)

    def finish(self):
        if self.late:
            self.across.finish()
        else:
            for made in self.far_own + self.far_other:
                made.wait_recv()

    def from_full(self):
        return list(self.far_own + tuple(self.across.first) if self.late else self.far_own + self.other + self.far_other)


class WeightSum:
    def __init__(self, links, part, relay, mid, last, other, expert, early):
        self.links, self.part, self.mid, self.last, self.other = links, part, mid, last, other
        self.expert, self.early = expert, early
        self.x, self.high, self.up, self.down, self.far = dp_places()
        if early:
            self.across = Across(links, relay, lambda way, to: other.at[:, pl.ds(64 * way, 64)])
            self.rows = self.high
        else:
            self.across = Across(links, relay, lambda way, to: other.at[pl.ds(64 * way, 64)])
            self.rows = pl.ds(0, 2)

    def towards(self, up, src, dst):
        return self.links.start(src, dst, dp=(self.up if up else self.down) * 2 + self.high)

    def x_start(self):
        e = self.expert
        self.far_up = self.towards(True, self.part.at[self.far, self.rows, e, pl.ds(0, 64)], self.mid.at[0])
        self.far_down = self.towards(False, self.part.at[self.far, self.rows, e, pl.ds(64, 64)], self.mid.at[1])

    def start(self):
        if self.early:
            self.across.start(
                [self.part.at[:, 1 - self.high, self.expert, pl.ds(64 * way, 64)] for way in range(2)]
            )
        else:
            self.x_start()

    def y_pass(self):
        self.across.pass_on()

    def y_add(self):
        self.across.finish()
        e, high = self.expert, self.high
        for x in range(4):
            self.part[x, high, e] = (self.part[x, high, e].astype(F32) + self.other[x].astype(F32)).astype(BF16)
        self.x_start()

    def add_mid(self, slot, place):
        rows = pl.ds(slot * 64, 64)
        for y in range(1 if self.early else 2):
            high = self.high if self.early else y
            mid = self.mid[slot] if self.early else self.mid[slot, y]
            self.part[place, high, self.expert, rows, :] = (
                mid.astype(F32) + self.part[place, high, self.expert, rows, :].astype(F32)
            ).astype(BF16)

    def pass_on(self):
        e = self.expert
        self.far_up.wait_recv()
        self.add_mid(0, self.up)
        self.to_up = self.towards(True, self.part.at[self.up, self.rows, e], self.last.at[0])
        self.far_down.wait_recv()
        self.add_mid(1, self.down)
        self.to_down = self.towards(False, self.part.at[self.down, self.rows, e], self.last.at[1])

    def chip(self, high):
        last = [self.last[way] if self.early else self.last[way, high] for way in range(2)]
        return last[0].astype(F32) + last[1].astype(F32) + self.part[self.x, high, self.expert].astype(F32)

    def y_start(self):
        high = 1 - self.high
        self.to_up.wait_recv()
        self.to_down.wait_recv()
        self.last[0, high] = self.chip(high).astype(BF16)
        self.across.start([self.last.at[0, high, pl.ds(64 * way, 64)] for way in range(2)])

    def finish(self, gateup, down):
        e = self.expert
        if self.early:
            self.to_up.wait_recv()
            self.to_down.wait_recv()
            value = self.chip(self.high)
        else:
            self.across.finish()
            value = self.chip(self.high) + self.other[...].astype(F32)
        gateup[e] = value[:, : 2 * FH]
        down[e, 0:128, :] = value[:, 2 * FH : 2 * FH + 128]
        down[e, 128:256, :] = value[:, 2 * FH + 128 :]


def exchange(links, source, target, axis):
    me = lax.axis_index(axis)
    copies = []
    for step in range(1, 8):
        to = lax.rem(me + step, 8)
        copies.append(links.start(source.at[to], target.at[me], **{axis: to}))
    target[me] = source[me]
    return copies


def column(row, rows, first):
    shape = (rows, row.shape[1])
    hit = lax.broadcasted_iota(jnp.int32, shape, 1) == lax.broadcasted_iota(jnp.int32, shape, 0) + first
    return jnp.sum(jnp.where(hit, row, 0.0), axis=1, keepdims=True)


def layer_kernel(x_ref, cot_ref, ids_ref, gates_ref, seg_ref, gains_own_ref, wq_ref, wkv_ref, wout_own_ref, wgu_ref,
                 wd_ref, ctab_ref, stab_ref, cfirst_ref, sfirst_ref,
                 out_ref, gradx_ref, gq_ref, gkv_ref, gains_ref, gout_ref, outgu_ref, outd_ref,
                 dense_own_ref, dense_ref, wouts_ref, pack_ref, full_ref, xs_ref, gr_ref, h2_ref,
                 near_ref, mid_ref, last_ref, pairs_ref, w_ref, h_ref, q_ref, kv_ref, o_ref,
                 segcol_ref, slot_ref, gate_ref, gatecol_ref, pick_ref, arrived_ref, dy_ref, hidden_ref, dgu_ref,
                 slots_ref, relay_p_ref, relay_q_ref, gmid_p_ref, gmid_q_ref,
                 glast_p_ref, glast_q_ref, gother_p_ref, gother_q_ref, oall_ref, dosend_ref, do_ref, dkv_ref, dqkv_ref,
                 gosend_ref, goswap_ref, goparts_ref, gwsend_ref, gwparts_ref, csend_ref, cparts_ref,
                 send_sem, recv_sem):
    dp, ctx, tensor = lax.axis_index("dp"), lax.axis_index("ctx"), lax.axis_index("tensor")
    own_lanes = pl.ds(pl.multiple_of(ctx * 128, 128), 128)
    dense_own_ref[0:128, 0:128] = wq_ref[:, own_lanes]
    dense_own_ref[0:128, 128:256] = wkv_ref[:, own_lanes]
    dense_own_ref[128:144, :] = jnp.zeros((16, 256), BF16)
    dense_own_ref[128:144, 0:128] = jnp.concatenate(
        [gains_own_ref[...].astype(F32), jnp.zeros((14, 128), F32)], axis=0
    ).astype(BF16)
    pack_ref[:, :, 0 : 2 * FH] = wgu_ref[...]
    pack_ref[:, :, 2 * FH : 2 * FH + 128] = wd_ref[:, 0:128, :]
    pack_ref[:, :, 2 * FH + 128 :] = wd_ref[:, 128:256, :]
    greet()
    links = Links(send_sem, recv_sem)
    rows_x = RowGather(links, xs_ref)
    rows_x.start(x_ref)
    dense = [links.start(dense_own_ref, dense_ref.at[dp], dp=lax.rem(dp + step, 8)) for step in range(1, 8)]
    swapped_in = links.copy(wout_own_ref, wouts_ref.at[dp], dp=ctx, ctx=dp)

    @pl.when(dp != ctx)
    def _():
        swapped_in.start()

    @pl.when(dp == ctx)
    def _():
        wouts_ref[ctx] = wout_own_ref[...]

    gathers = [
        WeightGather(links, full_ref, relay_q_ref.at[0, e] if e < LATE else relay_p_ref.at[0, e - LATE], e, e < LATE)
        for e in range(LOCAL_EXPERTS)
    ]
    late, soon = gathers[:LATE], gathers[LATE:]
    for gather in gathers:
        gather.start(pack_ref.at[gather.expert])
    xs_ref[ctx] = x_ref[...]
    dense_ref[dp] = dense_own_ref[...]
    full_ref[dp // 2, lax.rem(dp, 2)] = pack_ref[...]
    gr_ref[ctx] = cot_ref[...]

    segrow = seg_ref[...].astype(F32)
    for b in range(T // 128):
        segcol_ref[b * 128 : (b + 1) * 128, :] = column(segrow[:, b * 128 : (b + 1) * 128], 128, 0)
    chosen = []
    for k in range(LOCAL_EXPERTS):
        match = ids_ref[...] == ctx * LOCAL_EXPERTS + k
        chosen.append(jnp.sum(match.astype(F32), axis=0, keepdims=True))
        gate_ref[k : k + 1, :] = jnp.sum(jnp.where(match, gates_ref[...], 0.0), axis=0, keepdims=True)
    chosen = jnp.concatenate(chosen + [jnp.zeros((8 - LOCAL_EXPERTS, T), F32)], axis=0)
    earlier = lax.broadcasted_iota(jnp.int32, (128, 128), 0) < lax.broadcasted_iota(jnp.int32, (128, 128), 1)
    earlier = earlier.astype(F32).astype(BF16)
    for b in range(N_CTX):
        lanes = slice(b * 128, (b + 1) * 128)
        rank = dot(chosen[:, lanes].astype(BF16), earlier) + float(b % 2 * CAP)
        slot_ref[:, lanes] = jnp.where(chosen[:, lanes] > 0.5, rank, -1.0)

    rows_x.pass_on()
    place = lax.broadcasted_iota(jnp.int32, (SLOTS, BLOCK), 0).astype(F32)
    for pair in range(PAIRS):
        lanes = slice(pair * BLOCK, (pair + 1) * BLOCK)
        for k in range(LOCAL_EXPERTS):
            match = place == slot_ref[k : k + 1, lanes]
            pick_ref[pair, k * SLOTS : (k + 1) * SLOTS, :] = match.astype(F32).astype(BF16)
            gatecol_ref[k, pair * SLOTS : (pair + 1) * SLOTS, :] = jnp.sum(
                jnp.where(match, gate_ref[k : k + 1, lanes], 0.0), axis=1, keepdims=True
            )
    for gather in soon:
        gather.y_pass()
    rows_x.pass_far()
    def tables(rows):
        segcol = segcol_ref[rows, :]
        cfirst, sfirst = jnp.zeros((BLOCK, 128), F32), jnp.zeros((BLOCK, 128), F32)
        for d in range(5):
            cfirst = jnp.where(segcol == float(d), cfirst_ref[d : d + 1, :], cfirst)
            sfirst = jnp.where(segcol == float(d), sfirst_ref[d : d + 1, :], sfirst)
        ctab, stab = ctab_ref[rows, :], stab_ref[rows, :]
        sin = stab * cfirst - ctab * sfirst
        lane = lax.broadcasted_iota(jnp.int32, sin.shape, 1)
        return ctab * cfirst + stab * sfirst, jnp.where(lane % HD < HD // 2, -sin, sin)

    for made in dense:
        made.wait_recv()
    for k in range(N_DP):
        w_ref[k * 128 : (k + 1) * 128, :] = dense_ref[k, 0:128, :]
    gains = [
        jnp.concatenate([dense_ref[k, 128:144, 0:128] for k in range(N_DP)], axis=1).astype(F32)[n : n + 1]
        for n in range(2)
    ]
    rows_x.finish()

    @pl.when(dp != ctx)
    def _():
        swapped_in.wait_recv()

    rows_wout = RowGather(links, wouts_ref)
    rows_wout.start(wouts_ref.at[ctx])

    for r in range(T // BLOCK):
        rows = pl.ds(r * BLOCK, BLOCK)
        h = rms_norm(xs_ref[2 * r : 2 * r + 2].reshape(BLOCK, D).astype(F32), gains[0]).astype(BF16)
        h_ref[rows, :] = h
        qkv = dot(h, w_ref[...])
        cos, sin = tables(rows)
        query = qkv[:, :128]
        q_ref[rows, :] = (query * cos + swap_halves(query) * sin).astype(BF16)
        pair = qkv[:, 128:]
        turned = pair * cos + swap_halves(pair) * sin
        kv_ref[rows, :] = jnp.where(low_lanes(pair.shape), turned, pair).astype(BF16)

    rows_wout.pass_on()
    rows_gr = RowGather(links, gr_ref)
    rows_gr.start(cot_ref)
    low = low_lanes((BLOCK, 128))
    for r in range(T // BLOCK):
        rows = pl.ds(r * BLOCK, BLOCK)
        count = (r + 1) * BLOCK
        kv = kv_ref[0:count, :]
        query = q_ref[rows, :].astype(F32) * SCALE
        allowed = (segcol_ref[rows, :] == segrow[:, 0:count]) & (
            lax.broadcasted_iota(jnp.int32, (BLOCK, count), 0) + r * BLOCK
            >= lax.broadcasted_iota(jnp.int32, (BLOCK, count), 1)
        )
        outs = []
        for g in range(2):
            placed = query if g == 0 else pltpu.roll(query, HD, 1)
            placed = jnp.where(low, placed, 0.0).astype(BF16)
            scores = jnp.where(allowed, dot(placed, kv, ((1,), (1,))), NEGATIVE)
            largest = jnp.max(scores, axis=-1, keepdims=True)
            expon = jnp.exp(scores - largest)
            probs = (expon * (1.0 / jnp.sum(expon, axis=-1, keepdims=True))).astype(BF16)
            outs.append(dot(probs, kv))
        o_ref[2 * r : 2 * r + 2] = (
            jnp.where(low, pltpu.roll(outs[0], HD, 1), outs[1]).astype(BF16).reshape(2, 128, 128)
        )
        if r == 0:
            for gather in late:
                gather.pass_own()
        if r == 1:
            rows_wout.pass_far()
            soon[0].pass_other()
        if r == 2:
            for gather in late:
                gather.y_start()
    outputs = exchange(links, o_ref, oall_ref, "ctx")
    rows_gr.pass_on()
    for gather in soon:
        gather.pass_own()
    for gather in soon[1:]:
        gather.pass_other()
    rows_wout.finish()
    for made in outputs:
        made.wait_recv()
    attended = jnp.concatenate([oall_ref[k] for k in range(N_CTX)], axis=1)
    x2 = x_ref[...].astype(F32) + dot(attended, wouts_ref[...].reshape(D, D))
    h2_ref[ctx] = rms_norm(x2, gains[1]).astype(BF16)
    rows_h2 = RowGather(links, h2_ref)
    rows_h2.start(h2_ref.at[ctx])
    for gather in late:
        gather.y_pass()
    rows_gr.pass_far()
    rows_h2.pass_on()
    soon[0].pass_last()
    rows_gr.finish()
    for pair in range(PAIRS):
        grads = dot(pick_ref[pair], gr_ref[2 * pair : 2 * pair + 2].reshape(BLOCK, D))
        for k in range(LOCAL_EXPERTS):
            here = slice(pair * SLOTS, (pair + 1) * SLOTS)
            dy_ref[k, here, :] = (grads[k * SLOTS : (k + 1) * SLOTS] * gatecol_ref[k, here, :]).astype(BF16)
    rows_h2.pass_far()
    for gather in soon[1:]:
        gather.pass_last()
    rows_h2.finish()
    for pair in range(PAIRS):
        tokens = dot(pick_ref[pair], h2_ref[2 * pair : 2 * pair + 2].reshape(BLOCK, D)).astype(BF16)
        for k in range(LOCAL_EXPERTS):
            arrived_ref[k, pair * SLOTS : (pair + 1) * SLOTS, :] = tokens[k * SLOTS : (k + 1) * SLOTS]

    def down_of(e):
        return jnp.concatenate(
            [
                jnp.concatenate([full_ref[k // 2, k % 2, e, :, first : first + 128] for k in range(N_DP)], axis=1)
                for first in (2 * FH, 2 * FH + 128)
            ],
            axis=0,
        )

    def token_grads(e):
        gathers[e].finish()
        wgu = full_ref[:, :, e, :, 0 : 2 * FH].reshape(D, 2 * FH)
        gate_up = dot(arrived_ref[e], wgu)
        gate, up = gate_up[:, :FH], gate_up[:, FH:]
        sigma = jax.nn.sigmoid(gate)
        silu = gate * sigma
        hidden_ref[e] = (silu * up).astype(BF16)
        grad_hidden = dot(dy_ref[e], down_of(e), ((1,), (1,)))
        grad_gate = grad_hidden * up * (sigma * (1.0 + gate * (1.0 - sigma)))
        dgu_ref[e] = jnp.concatenate([grad_gate, grad_hidden * silu], axis=1).astype(BF16)
        back = dot(dgu_ref[e], wgu, ((1,), (1,))).astype(BF16)
        for pair in range(PAIRS):
            slots_ref[pair, e * SLOTS : (e + 1) * SLOTS, :] = back[pair * SLOTS : (pair + 1) * SLOTS]

    weights = [
        WeightSum(links, full_ref, relay_q_ref.at[1, e], gmid_q_ref.at[e], glast_q_ref.at[e], gother_q_ref.at[e], e, True)
        if e < LATE
        else WeightSum(
            links, full_ref, relay_p_ref.at[1, e - LATE], gmid_p_ref.at[e - LATE], glast_p_ref.at[e - LATE],
            gother_p_ref.at[e - LATE], e, False,
        )
        for e in range(LOCAL_EXPERTS)
    ]

    def weight_grads(e):
        hidden, dy = hidden_ref[e], dy_ref[e]
        out = (dot(hidden, down_of(e)) * gatecol_ref[e]).astype(BF16)
        grad_down = dot(hidden, dy, ((0,), (0,))).astype(BF16)
        dy_ref[e] = out
        links.settle(gathers[e].from_full())
        for k in range(N_DP):
            lanes = slice(k * 128, (k + 1) * 128)
            full_ref[k // 2, k % 2, e, :, 2 * FH : 2 * FH + 128] = grad_down[0:128, lanes]
            full_ref[k // 2, k % 2, e, :, 2 * FH + 128 :] = grad_down[128:256, lanes]
        grad_gateup = dot(arrived_ref[e], dgu_ref[e], ((0,), (0,))).astype(BF16)
        full_ref[:, :, e, :, 0 : 2 * FH] = grad_gateup.reshape(4, 2, 128, 2 * FH)
        weights[e].start()

    early, after = weights[:LATE], weights[LATE:]
    order = [2, 0, 3, 1]
    token_grads(order[0])
    token_grads(order[1])
    weight_grads(order[0])
    token_grads(order[2])
    weight_grads(order[1])
    token_grads(order[3])
    links.settle(rows_x.all())
    sum_dh2 = RowSum(links, xs_ref, near_ref.at[1], mid_ref.at[1], last_ref.at[1])
    for pair in range(PAIRS):
        rows_back = dot(pick_ref[pair], slots_ref[pair], ((0,), (0,))).astype(BF16)
        xs_ref[2 * pair : 2 * pair + 2] = rows_back.reshape(2, 128, D)
        sum_dh2.send(pair)
    weight_grads(order[2])
    sum_dh2.pair()
    weights[2].pass_on()
    weights[0].y_pass()
    weight_grads(order[3])
    sum_dh2.pass_on()
    links.settle(rows_gr.all())
    sum_y = RowSum(links, gr_ref, near_ref.at[2], mid_ref.at[2], last_ref.at[2])
    for pair in range(PAIRS):
        slot_rows = jnp.concatenate(
            [dy_ref[k, pair * SLOTS : (pair + 1) * SLOTS, :] for k in range(LOCAL_EXPERTS)], axis=0
        )
        rows_out = dot(pick_ref[pair], slot_rows, ((0,), (0,))).astype(BF16)
        gr_ref[2 * pair : 2 * pair + 2] = rows_out.reshape(2, 128, D)
        sum_y.send(pair)
    pairs_ref[0] = sum_dh2.finish().astype(BF16)
    swap = links.start(pairs_ref.at[0], pairs_ref.at[1], tensor=1 - tensor)
    sum_y.pair()
    weights[3].pass_on()
    weights[1].y_pass()
    inverse = lax.rsqrt(jnp.mean(x2 * x2, axis=-1, keepdims=True) + EPSILON)
    scaled = x2 * inverse
    swap.wait_recv()
    dh2 = pairs_ref[0].astype(F32) + pairs_ref[1].astype(F32)
    weighted = dh2 * gains[1]
    dx2 = cot_ref[...].astype(F32) + inverse * (
        weighted - scaled * jnp.mean(weighted * scaled, axis=-1, keepdims=True)
    )
    gradx_ref[...] = dx2
    da = dx2.astype(BF16)
    grad_heads = dot(da, wouts_ref[...].reshape(D, D), ((1,), (1,))).astype(BF16)
    for k in range(N_CTX):
        dosend_ref[k] = grad_heads[:, k * 128 : (k + 1) * 128]
    grad_outputs = exchange(links, dosend_ref, do_ref, "ctx")
    gain_two = jnp.sum(dh2 * scaled, axis=0, keepdims=True)
    gwsend_ref[:, 128:144, :] = jnp.zeros((N_DP, 16, 256), BF16)
    for k in range(N_DP):
        gwsend_ref[k, 128:144, 0:128] = jnp.broadcast_to(gain_two[:, k * 128 : (k + 1) * 128], (16, 128)).astype(BF16)
    sum_y.pass_on()
    links.settle(rows_h2.all())
    sum_out = RowSum(links, h2_ref, near_ref.at[0], mid_ref.at[0], last_ref.at[0])
    for k in range(N_CTX):
        h2_ref[k] = dot(oall_ref[k], da, ((0,), (0,))).astype(BF16)
    for z in range(4):
        sum_out.send(z)
    weights[0].y_add()
    for made in grad_outputs:
        made.wait_recv()
    sum_out.pair()
    dkv_ref[...] = jnp.zeros_like(dkv_ref)
    links.settle(sum_dh2.sent)
    sum_dh = RowSum(links, xs_ref, near_ref.at[3], mid_ref.at[3], last_ref.at[3])
    for r in reversed(range(T // BLOCK)):
        rows = pl.ds(r * BLOCK, BLOCK)
        count = (r + 1) * BLOCK
        kv = kv_ref[0:count, :]
        query = q_ref[rows, :].astype(F32) * SCALE
        grad = do_ref[2 * r : 2 * r + 2].reshape(BLOCK, 128).astype(F32)
        allowed = (segcol_ref[0:count, :] == segrow[:, r * BLOCK : (r + 1) * BLOCK]) & (
            lax.broadcasted_iota(jnp.int32, (count, BLOCK), 1) + r * BLOCK
            >= lax.broadcasted_iota(jnp.int32, (count, BLOCK), 0)
        )
        grads = []
        for g in range(2):
            placed = query if g == 0 else pltpu.roll(query, HD, 1)
            placed = jnp.where(low, placed, 0.0).astype(BF16)
            placed_grad = grad if g == 1 else pltpu.roll(grad, HD, 1)
            placed_grad = jnp.where(low, 0.0, placed_grad).astype(BF16)
            scores = jnp.where(allowed, dot(kv, placed, ((1,), (1,))), NEGATIVE)
            largest = jnp.max(scores, axis=0, keepdims=True)
            expon = jnp.exp(scores - largest)
            probs = expon * (1.0 / jnp.sum(expon, axis=0, keepdims=True))
            grad_probs = dot(kv, placed_grad, ((1,), (1,)))
            delta = jnp.sum(grad_probs * probs, axis=0, keepdims=True)
            grad_scores = (probs * (grad_probs - delta)).astype(BF16)
            dkv_ref[0:count, :] += dot(grad_scores, placed) + dot(probs.astype(BF16), placed_grad)
            grads.append(dot(grad_scores, kv, ((0,), (0,))) * SCALE)
        grad_query = jnp.where(low, grads[0], pltpu.roll(grads[1], HD, 1))
        cos, sin = tables(rows)
        dqkv_ref[rows, 0:128] = (grad_query * cos - swap_halves(grad_query) * sin).astype(BF16)
        grad_pair = dkv_ref[rows, :]
        turned = grad_pair * cos - swap_halves(grad_pair) * sin
        dqkv_ref[rows, 128:256] = jnp.where(low, turned, grad_pair).astype(BF16)
        dh_part = dot(dqkv_ref[rows, :], w_ref[...], ((1,), (1,))).astype(BF16)
        xs_ref[2 * r : 2 * r + 2] = dh_part.reshape(2, 128, D)
        sum_dh.send(r)
        if r == 3:
            sum_out.pass_on()
            weights[1].y_add()
            weights[2].y_start()
        if r == 2:
            pairs_ref[2] = sum_y.finish().astype(BF16)
            swap_y = links.start(pairs_ref.at[2], pairs_ref.at[3], tensor=1 - tensor)
            weights[0].pass_on()
            weights[3].y_start()
        if r == 1:
            weights[2].y_pass()
            gosend_ref[...] = sum_out.finish().astype(BF16).reshape(N_CTX, 16, D)
            swapped = links.copy(gosend_ref, goswap_ref, dp=ctx, ctx=dp)

            @pl.when(dp != ctx)
            def _():
                swapped.start()

            @pl.when(dp == ctx)
            def _():
                goswap_ref[...] = gosend_ref[...]

    gw = dot(h_ref[...], dqkv_ref[...], ((0,), (0,)))
    gwsend_ref[:, 0:128, :] = gw.astype(BF16).reshape(N_DP, 128, 256)
    gwparts = exchange(links, gwsend_ref, gwparts_ref, "dp")
    sum_dh.pair()
    weights[1].pass_on()
    weights[3].y_pass()

    @pl.when(dp != ctx)
    def _():
        swapped.wait_recv()

    goparts = exchange(links, goswap_ref, goparts_ref, "ctx")
    sum_dh.pass_on()
    for made in gwparts:
        made.wait_recv()
    mine = gwparts_ref[0].astype(F32)
    for k in range(1, N_DP):
        mine += gwparts_ref[k].astype(F32)
    for k in range(N_CTX):
        csend_ref[k, 0:16, :] = mine[k * 16 : (k + 1) * 16]
        csend_ref[k, 16:24, :] = mine[128:136]
    cparts = exchange(links, csend_ref, cparts_ref, "ctx")
    dh = sum_dh.finish()
    x_own = x_ref[...].astype(F32)
    inverse = lax.rsqrt(jnp.mean(x_own * x_own, axis=-1, keepdims=True) + EPSILON)
    scaled = x_own * inverse
    weighted = dh * gains[0]
    gradx_ref[...] += inverse * (weighted - scaled * jnp.mean(weighted * scaled, axis=-1, keepdims=True))
    for made in goparts:
        made.wait_recv()
    total_out = goparts_ref[0].astype(F32)
    for k in range(1, N_CTX):
        total_out += goparts_ref[k].astype(F32)
    gout_ref[...] = total_out
    swap_y.wait_recv()
    out_ref[...] = (x2 + (pairs_ref[2].astype(F32) + pairs_ref[3].astype(F32))).astype(BF16)
    for each in (weights[2], weights[0]):
        each.finish(outgu_ref, outd_ref)
    for made in cparts:
        made.wait_recv()
    gain_row = cparts_ref[0, 16:24, 0:128]
    for k in range(N_CTX):
        gq_ref[:, k * 128 : (k + 1) * 128] = cparts_ref[k, 0:16, 0:128]
        gkv_ref[:, k * 128 : (k + 1) * 128] = cparts_ref[k, 0:16, 128:256]
        if k > 0:
            gain_row += cparts_ref[k, 16:24, 0:128]
    own_rows = pl.ds(pl.multiple_of(ctx * 16, 16), 16)
    gain_one = jnp.sum(
        wq_ref[own_rows, :].astype(F32) * gq_ref[...] + wkv_ref[own_rows, :].astype(F32) * gkv_ref[...],
        axis=1,
        keepdims=True,
    ) / column(gains_own_ref[...].astype(F32)[0:1], 16, ctx * 16)
    gain_two = column(gain_row[0:1], 16, ctx * 16)
    lane = lax.broadcasted_iota(jnp.int32, (16, 128), 1)
    gains_ref[...] = jnp.where(lane == 0, gain_one, gain_two)
    for each in (weights[3], weights[1]):
        each.finish(outgu_ref, outd_ref)
    links.finish((swapped, swapped_in))

    @pl.when(dp != ctx)
    def _():
        swapped.wait_send()
        swapped_in.wait_send()


def layer(*args):
    shapes = [
        ((ROWS, D), BF16), ((ROWS, D), F32), ((16, D), F32), ((16, D), F32), ((16, 128), F32), ((16, D), F32),
        ((LOCAL_EXPERTS, 128, 2 * FH), F32), ((LOCAL_EXPERTS, FH, 128), F32),
    ]
    blocks = (N_CTX, ROWS, D)
    capacity = PAIRS * SLOTS
    scratch = [
        ((144, 256), BF16), ((N_DP, 144, 256), BF16), (blocks, BF16), ((LOCAL_EXPERTS, 128, WIDE), BF16),
        ((4, 2, LOCAL_EXPERTS, 128, WIDE), BF16), (blocks, BF16), (blocks, BF16), (blocks, BF16),
        ((4, 4, ROWS, D), BF16), ((4, 2, ROWS // 2, D), BF16), ((4, 2, ROWS, D), BF16), ((4, ROWS, D), BF16),
        ((D, 256), BF16), ((T, D), BF16), ((T, 128), BF16), ((T, 128), BF16), ((N_CTX, 128, 128), BF16),
        ((T, 1), F32), ((8, T), F32), ((LOCAL_EXPERTS, T), F32), ((LOCAL_EXPERTS, capacity, 1), F32),
        ((PAIRS, LOCAL_EXPERTS * SLOTS, BLOCK), BF16), ((LOCAL_EXPERTS, capacity, D), BF16),
        ((LOCAL_EXPERTS, capacity, D), BF16), ((LOCAL_EXPERTS, capacity, FH), BF16),
        ((LOCAL_EXPERTS, capacity, 2 * FH), BF16),
        ((PAIRS, LOCAL_EXPERTS * SLOTS, D), BF16),
        ((2, SOON, 2, 64, WIDE), BF16), ((2, LATE, 2, 4, 64, WIDE), BF16),
        ((SOON, 2, 2, 64, WIDE), BF16), ((LATE, 2, 64, WIDE), BF16),
        ((SOON, 2, 2, 128, WIDE), BF16), ((LATE, 2, 128, WIDE), BF16),
        ((SOON, 128, WIDE), BF16), ((LATE, 4, 128, WIDE), BF16), ((N_CTX, 128, 128), BF16), ((N_CTX, 128, 128), BF16),
        ((N_CTX, 128, 128), BF16),
        ((T, 128), F32), ((T, 256), BF16),
        ((N_CTX, 16, D), BF16), ((N_CTX, 16, D), BF16), ((N_CTX, 16, D), BF16), ((N_DP, 144, 256), BF16),
        ((N_DP, 144, 256), BF16), ((N_CTX, 24, 256), F32), ((N_CTX, 24, 256), F32),
    ]
    return pl.pallas_call(
        layer_kernel,
        out_shape=[jax.ShapeDtypeStruct(s, t) for s, t in shapes],
        in_specs=[pl.BlockSpec(memory_space=pltpu.VMEM)] * len(args),
        out_specs=[pl.BlockSpec(memory_space=pltpu.VMEM)] * len(shapes),
        scratch_shapes=[pltpu.VMEM(s, t) for s, t in scratch]
        + [pltpu.SemaphoreType.DMA((COPIES,)), pltpu.SemaphoreType.DMA((COPIES,))],
        compiler_params=pltpu.CompilerParams(
            vmem_limit_bytes=VMEM_LIMIT, collective_id=0, has_side_effects=True
        ),
        cost_estimate=pl.CostEstimate(flops=20_000_000_000, bytes_accessed=10_000_000, transcendentals=4_000_000),
        name="layer",
    )(*args)


def on_device(
    activations, cotangent, segment_ids, expert_ids, gate_weights, norm_gains, w_query, w_keyval, w_out, w_gateup, w_down
):
    frequency = np.exp(np.arange(HD // 2, dtype=np.float32) * np.float32(-2.0 * math.log(10000.0) / HD))
    frequency = np.tile(frequency.astype(np.float32), 4)[None, :]
    angles = (np.arange(T, dtype=np.float32)[:, None] * frequency).astype(np.float64)
    ctab, stab = np.cos(angles).astype(np.float32), np.sin(angles).astype(np.float32)
    documents = jnp.arange(8, dtype=jnp.int32)[:, None]
    first = jnp.sum((segment_ids < documents).astype(jnp.int32), axis=1, keepdims=True).astype(F32)
    out, grad_x, gq, gkv, gains, gout, grad_gateup, grad_down = layer(
        activations, cotangent, expert_ids[0].T, gate_weights[0].T, segment_ids, norm_gains[0], w_query[0], w_keyval[0],
        w_out[0], w_gateup[0].reshape(LOCAL_EXPERTS, 128, 2 * FH), w_down[0], jnp.asarray(ctab), jnp.asarray(stab),
        jnp.cos(first * frequency), jnp.sin(first * frequency),
    )
    return (
        out,
        grad_x,
        gains[:, 0:2].T[None],
        gq[None],
        gkv[None],
        gout[None],
        grad_gateup.reshape(1, LOCAL_EXPERTS, 128, 2, FH),
        grad_down[None],
    )


def solution(mesh):
    return jax.shard_map(
        on_device,
        mesh=mesh,
        in_specs=(
            P(("dp", "ctx"), None),
            P(("dp", "ctx"), None),
            P("dp", None),
            P(None, "dp", None),
            P(None, "dp", None),
            P(None, None, "dp"),
            P(None, "dp", None),
            P(None, "dp", None),
            P(None, "dp", None),
            P(None, "ctx", "dp", None, "tensor"),
            P(None, "ctx", "tensor", "dp"),
        ),
        out_specs=(
            P(("dp", "ctx"), None),
            P(("dp", "ctx"), None),
            P(None, None, ("dp", "ctx")),
            P(None, ("dp", "ctx"), None),
            P(None, ("dp", "ctx"), None),
            P(None, ("dp", "ctx"), None),
            P(None, "ctx", "dp", None, "tensor"),
            P(None, "ctx", "tensor", "dp"),
        ),
        check_vma=False,
    )
```

```python
import math

import jax
import jax.numpy as jnp
import numpy as np
from jax import lax
from jax.experimental import pallas as pl
from jax.experimental.pallas import tpu as pltpu
from jax.sharding import PartitionSpec as P

D = 1024
HD = 64
T = 1024
ROWS = 128
N_DP = 8
N_CTX = 8
LOCAL_EXPERTS = 4
CAP = 40
PAIRS = 4
SLOTS = 2 * CAP
FH = 256
BLOCK = 256
EPSILON = 1e-06
NEGATIVE = -1e30
SCALE = 1.0 / math.sqrt(HD)
BF16 = jnp.bfloat16
F32 = jnp.float32
VMEM_LIMIT = 62 * 1024 * 1024
WIDE = 2 * FH + 256
LATE = 1
SOON = LOCAL_EXPERTS - LATE
COPIES = 224


def dot(a, b, dims=((1,), (0,))):
    return lax.dot_general(a, b, (dims, ((), ())), preferred_element_type=F32)


def rms_norm(values, gain):
    return values * lax.rsqrt(jnp.mean(values * values, axis=-1, keepdims=True) + EPSILON) * gain


def swap_halves(values):
    lane = lax.broadcasted_iota(jnp.int32, values.shape, 1)
    return jnp.where(lane % HD < HD // 2, pltpu.roll(values, 96, 1), pltpu.roll(values, 32, 1))


def low_lanes(shape):
    return lax.broadcasted_iota(jnp.int32, shape, 1) < HD


class Links:
    def __init__(self, send, recv):
        self.send, self.recv, self.made, self.settled = send, recv, [], []

    def copy(self, src, dst, **device):
        place = len(self.made)
        assert place < COPIES
        made = pltpu.make_async_remote_copy(
            src_ref=src,
            dst_ref=dst,
            send_sem=self.send.at[place],
            recv_sem=self.recv.at[place],
            device_id=device,
            device_id_type=pl.DeviceIdType.MESH,
        )
        self.made.append(made)
        return made

    def start(self, src, dst, **device):
        made = self.copy(src, dst, **device)
        made.start()
        return made

    def settle(self, copies):
        for made in copies:
            made.wait_send()
            self.settled.append(id(made))

    def finish(self, skip=()):
        for made in self.made:
            if id(made) not in self.settled and not any(made is each for each in skip):
                made.wait_send()


def ctx_places():
    me = lax.axis_index("ctx")
    z, core = me // 2, me % 2
    at = lambda step: lax.rem(z + step, 4) * 2 + core
    return me, z * 2 + 1 - core, at(1), at(3), at(2)


def dp_places():
    me = lax.axis_index("dp")
    x, high = me // 2, me % 2
    at = lambda step: lax.rem(x + step, 4)
    return x, high, at(1), at(3), at(2)


class RowGather:
    def __init__(self, links, full):
        self.links, self.full = links, full
        self.me, self.sib, self.up, self.down, self.far = ctx_places()

    def start(self, own):
        full, mine = self.full, self.full.at[self.me]
        half = full.shape[1] // 2
        first, rest = pl.ds(0, half), pl.ds(half, half)
        self.to_up = self.links.start(own.at[first], mine.at[first], ctx=self.up)
        self.to_down = self.links.start(own.at[rest], mine.at[rest], ctx=self.down)
        self.rest_up = self.links.start(own.at[rest], mine.at[rest], ctx=self.up)
        self.rest_down = self.links.start(own.at[first], mine.at[first], ctx=self.down)
        self.to_sib = [self.links.start(own, mine, ctx=self.sib)]

    def pass_on(self):
        full, links = self.full, self.links
        half = full.shape[1] // 2
        self.to_up.wait_recv()
        part = full.at[self.down, pl.ds(0, half)]
        self.far_up = links.start(part, part, ctx=self.up)
        self.to_down.wait_recv()
        part = full.at[self.up, pl.ds(half, half)]
        self.far_down = links.start(part, part, ctx=self.down)
        for place, arrival in ((self.down, self.rest_up), (self.up, self.rest_down)):
            arrival.wait_recv()
            part = full.at[place]
            self.to_sib.append(links.start(part, part, ctx=self.sib))

    def pass_far(self):
        full, links = self.full, self.links
        half = full.shape[1] // 2
        for arrival, first in ((self.far_up, 0), (self.far_down, half)):
            arrival.wait_recv()
            part = full.at[self.far, pl.ds(first, half)]
            self.to_sib.append(links.start(part, part, ctx=self.sib))

    def all(self):
        return [self.to_up, self.to_down, self.rest_up, self.rest_down, self.far_up, self.far_down] + self.to_sib

    def finish(self):
        for made in self.to_sib:
            made.wait_recv()


class RowSum:
    def __init__(self, links, part, near, mid, last):
        self.links, self.part, self.near, self.mid, self.last = links, part, near, mid, last
        self.me, self.sib, self.up, self.down, self.far = ctx_places()
        self.core = self.me % 2
        self.sent = []

    def send(self, z):
        self.sent.append(self.links.start(self.part.at[2 * z + 1 - self.core], self.near.at[z], ctx=self.sib))

    def add(self, place):
        z = place // 2
        self.near[z] = (self.near[z].astype(F32) + self.part[2 * z + self.core].astype(F32)).astype(BF16)

    def pair(self):
        links, near, half = self.links, self.near, self.near.shape[1] // 2
        for made in self.sent:
            made.wait_recv()
        self.add(self.far)
        far = self.far // 2
        self.far_up = links.start(near.at[far, pl.ds(0, half)], self.mid.at[0], ctx=self.up)
        self.far_down = links.start(near.at[far, pl.ds(half, half)], self.mid.at[1], ctx=self.down)
        up, down = self.up // 2, self.down // 2
        self.add(self.up)
        self.rest_up = links.start(near.at[up, pl.ds(half, half)], self.last.at[0, pl.ds(half, half)], ctx=self.up)
        self.add(self.down)
        self.rest_down = links.start(near.at[down, pl.ds(0, half)], self.last.at[1, pl.ds(0, half)], ctx=self.down)
        self.add(self.me)

    def pass_on(self):
        links, near, half = self.links, self.near, self.near.shape[1] // 2
        up, down = self.up // 2, self.down // 2
        self.far_up.wait_recv()
        near[up, 0:half] = (near[up, 0:half].astype(F32) + self.mid[0].astype(F32)).astype(BF16)
        self.to_up = links.start(near.at[up, pl.ds(0, half)], self.last.at[0, pl.ds(0, half)], ctx=self.up)
        self.far_down.wait_recv()
        near[down, half:] = (near[down, half:].astype(F32) + self.mid[1].astype(F32)).astype(BF16)
        self.to_down = links.start(
            near.at[down, pl.ds(half, half)], self.last.at[1, pl.ds(half, half)], ctx=self.down
        )

    def finish(self):
        for made in (self.rest_up, self.rest_down, self.to_up, self.to_down):
            made.wait_recv()
        return self.near[self.me // 2].astype(F32) + (self.last[0].astype(F32) + self.last[1].astype(F32))


def greet():
    barrier = pltpu.get_barrier_semaphore()
    dp, ctx = lax.axis_index("dp"), lax.axis_index("ctx")

    def signal(**device):
        pl.semaphore_signal(barrier, inc=1, device_id=device, device_id_type=pl.DeviceIdType.MESH)

    for step in range(1, 8):
        signal(ctx=lax.rem(ctx + step, 8))
        signal(dp=lax.rem(dp + step, 8))
    signal(tensor=1 - lax.axis_index("tensor"))
    signal(dp=dp + 1 - 2 * lax.rem(dp, 2), tensor=1 - lax.axis_index("tensor"))

    @pl.when(dp != ctx)
    def _():
        signal(dp=ctx, ctx=dp)
        pl.semaphore_wait(barrier, 17)

    @pl.when(dp == ctx)
    def _():
        pl.semaphore_wait(barrier, 16)


def y_places():
    dp, tensor = lax.axis_index("dp"), lax.axis_index("tensor")
    same, other = dp, dp + 1 - 2 * lax.rem(dp, 2)
    up = jnp.where(tensor == 0, same, other)
    return up, same + other - up, 1 - tensor


class Across:
    def __init__(self, links, relay, target):
        self.links, self.relay, self.target = links, relay, target
        self.up, self.down, self.tensor = y_places()

    def start(self, halves):
        self.first = [
            self.links.start(halves[0], self.relay.at[0], dp=self.up, tensor=self.tensor),
            self.links.start(halves[1], self.relay.at[1], dp=self.down, tensor=self.tensor),
        ]

    def pass_on(self):
        self.second = []
        for way, to in ((0, self.up), (1, self.down)):
            self.first[way].wait_recv()
            self.second.append(
                self.links.start(self.relay.at[way], self.target(way, to), dp=to, tensor=self.tensor)
            )

    def finish(self):
        for made in self.second:
            made.wait_recv()


class WeightGather:
    def __init__(self, links, full, relay, expert, late):
        self.links, self.full, self.expert, self.late = links, full, expert, late
        self.x, self.high, self.up, self.down, self.far = dp_places()
        if late:
            target = lambda way, to: full.at[:, 1 - lax.rem(to, 2), expert, pl.ds(64 * way, 64)]
        else:
            target = lambda way, to: full.at[self.x, 1 - lax.rem(to, 2), expert, pl.ds(64 * way, 64)]
        self.across = Across(links, relay, target)

    def both(self, src, dst):
        return (
            self.links.start(src, dst, dp=self.up * 2 + self.high),
            self.links.start(src, dst, dp=self.down * 2 + self.high),
        )

    def start(self, own):
        self.own = self.both(own, self.full.at[self.x, self.high, self.expert])

    def start_across(self, own):
        self.across.start([own.at[pl.ds(64 * way, 64)] for way in range(2)])

    def relay(self, arrivals, high):
        arrivals[0].wait_recv()
        part = self.full.at[self.down, high, self.expert, pl.ds(0, 64)]
        first = self.links.start(part, part, dp=self.up * 2 + self.high)
        arrivals[1].wait_recv()
        part = self.full.at[self.up, high, self.expert, pl.ds(64, 64)]
        return first, self.links.start(part, part, dp=self.down * 2 + self.high)

    def pass_own(self):
        self.far_own = self.relay(self.own, self.high)

    def y_start(self):
        for made in self.far_own:
            made.wait_recv()
        self.across.start(
            [self.full.at[:, self.high, self.expert, pl.ds(64 * way, 64)] for way in range(2)]
        )

    def y_pass(self):
        self.across.pass_on()

    def pass_other(self):
        self.across.finish()
        part = self.full.at[self.x, 1 - self.high, self.expert]
        self.other = self.both(part, part)

    def pass_last(self):
        self.far_other = self.relay(self.other, 1 - self.high)

    def finish(self):
        if self.late:
            self.across.finish()
        else:
            for made in self.far_own + self.far_other:
                made.wait_recv()

    def from_full(self):
        return list(self.far_own + tuple(self.across.first) if self.late else self.far_own + self.other + self.far_other)


class WeightSum:
    def __init__(self, links, part, relay, mid, last, other, expert, early):
        self.links, self.part, self.mid, self.last, self.other = links, part, mid, last, other
        self.expert, self.early = expert, early
        self.x, self.high, self.up, self.down, self.far = dp_places()
        if early:
            self.across = Across(links, relay, lambda way, to: other.at[:, pl.ds(64 * way, 64)])
            self.rows = self.high
        else:
            self.across = Across(links, relay, lambda way, to: other.at[pl.ds(64 * way, 64)])
            self.rows = pl.ds(0, 2)

    def towards(self, up, src, dst):
        return self.links.start(src, dst, dp=(self.up if up else self.down) * 2 + self.high)

    def x_start(self):
        e = self.expert
        self.far_up = self.towards(True, self.part.at[self.far, self.rows, e, pl.ds(0, 64)], self.mid.at[0])
        self.far_down = self.towards(False, self.part.at[self.far, self.rows, e, pl.ds(64, 64)], self.mid.at[1])

    def start(self):
        if self.early:
            self.across.start(
                [self.part.at[:, 1 - self.high, self.expert, pl.ds(64 * way, 64)] for way in range(2)]
            )
        else:
            self.x_start()

    def y_pass(self):
        self.across.pass_on()

    def y_add(self):
        self.across.finish()
        e, high = self.expert, self.high
        for x in range(4):
            self.part[x, high, e] = (self.part[x, high, e].astype(F32) + self.other[x].astype(F32)).astype(BF16)
        self.x_start()

    def add_mid(self, slot, place):
        rows = pl.ds(slot * 64, 64)
        for y in range(1 if self.early else 2):
            high = self.high if self.early else y
            mid = self.mid[slot] if self.early else self.mid[slot, y]
            self.part[place, high, self.expert, rows, :] = (
                mid.astype(F32) + self.part[place, high, self.expert, rows, :].astype(F32)
            ).astype(BF16)

    def pass_on(self):
        e = self.expert
        self.far_up.wait_recv()
        self.add_mid(0, self.up)
        self.to_up = self.towards(True, self.part.at[self.up, self.rows, e], self.last.at[0])
        self.far_down.wait_recv()
        self.add_mid(1, self.down)
        self.to_down = self.towards(False, self.part.at[self.down, self.rows, e], self.last.at[1])

    def chip(self, high):
        last = [self.last[way] if self.early else self.last[way, high] for way in range(2)]
        return last[0].astype(F32) + last[1].astype(F32) + self.part[self.x, high, self.expert].astype(F32)

    def y_start(self):
        high = 1 - self.high
        self.to_up.wait_recv()
        self.to_down.wait_recv()
        self.last[0, high] = self.chip(high).astype(BF16)
        self.across.start([self.last.at[0, high, pl.ds(64 * way, 64)] for way in range(2)])

    def finish(self, gateup, down):
        e = self.expert
        if self.early:
            self.to_up.wait_recv()
            self.to_down.wait_recv()
            value = self.chip(self.high)
        else:
            self.across.finish()
            value = self.chip(self.high) + self.other[...].astype(F32)
        gateup[e] = value[:, : 2 * FH]
        down[e, 0:128, :] = value[:, 2 * FH : 2 * FH + 128]
        down[e, 128:256, :] = value[:, 2 * FH + 128 :]


def exchange(links, source, target, axis):
    me = lax.axis_index(axis)
    copies = []
    for step in range(1, 8):
        to = lax.rem(me + step, 8)
        copies.append(links.start(source.at[to], target.at[me], **{axis: to}))
    target[me] = source[me]
    return copies


def column(row, rows, first):
    shape = (rows, row.shape[1])
    hit = lax.broadcasted_iota(jnp.int32, shape, 1) == lax.broadcasted_iota(jnp.int32, shape, 0) + first
    return jnp.sum(jnp.where(hit, row, 0.0), axis=1, keepdims=True)


def layer_kernel(x_ref, cot_ref, ids_ref, gates_ref, seg_ref, gains_own_ref, wq_ref, wkv_ref, wout_own_ref, wgu_ref,
                 wd_ref, ctab_ref, stab_ref, cfirst_ref, sfirst_ref,
                 out_ref, gradx_ref, gq_ref, gkv_ref, gains_ref, gout_ref, outgu_ref, outd_ref,
                 dense_own_ref, dense_ref, wouts_ref, pack_ref, full_ref, xs_ref, gr_ref, h2_ref,
                 near_ref, mid_ref, last_ref, pairs_ref, w_ref, h_ref, q_ref, kv_ref, o_ref,
                 segcol_ref, slot_ref, gate_ref, gatecol_ref, pick_ref, arrived_ref, dy_ref, hidden_ref, dgu_ref,
                 slots_ref, relay_p_ref, relay_q_ref, gmid_p_ref, gmid_q_ref,
                 glast_p_ref, glast_q_ref, gother_p_ref, gother_q_ref, oall_ref, dosend_ref, do_ref, dkv_ref, dqkv_ref,
                 gosend_ref, goswap_ref, goparts_ref, gwsend_ref, gwparts_ref, csend_ref, cparts_ref,
                 send_sem, recv_sem):
    dp, ctx, tensor = lax.axis_index("dp"), lax.axis_index("ctx"), lax.axis_index("tensor")
    own_lanes = pl.ds(pl.multiple_of(ctx * 128, 128), 128)
    dense_own_ref[0:128, 0:128] = wq_ref[:, own_lanes]
    dense_own_ref[0:128, 128:256] = wkv_ref[:, own_lanes]
    dense_own_ref[128:144, :] = jnp.zeros((16, 256), BF16)
    dense_own_ref[128:144, 0:128] = jnp.concatenate(
        [gains_own_ref[...].astype(F32), jnp.zeros((14, 128), F32)], axis=0
    ).astype(BF16)
    pack_ref[:, :, 0 : 2 * FH] = wgu_ref[...]
    pack_ref[:, :, 2 * FH : 2 * FH + 128] = wd_ref[:, 0:128, :]
    pack_ref[:, :, 2 * FH + 128 :] = wd_ref[:, 128:256, :]
    greet()
    links = Links(send_sem, recv_sem)
    rows_x = RowGather(links, xs_ref)
    rows_x.start(x_ref)
    dense = [links.start(dense_own_ref, dense_ref.at[dp], dp=lax.rem(dp + step, 8)) for step in range(1, 8)]
    swapped_in = links.copy(wout_own_ref, wouts_ref.at[dp], dp=ctx, ctx=dp)

    @pl.when(dp != ctx)
    def _():
        swapped_in.start()

    @pl.when(dp == ctx)
    def _():
        wouts_ref[ctx] = wout_own_ref[...]

    gathers = [
        WeightGather(links, full_ref, relay_q_ref.at[0, e] if e < LATE else relay_p_ref.at[0, e - LATE], e, e < LATE)
        for e in range(LOCAL_EXPERTS)
    ]
    late, soon = gathers[:LATE], gathers[LATE:]
    for gather in gathers[:2]:
        gather.start(pack_ref.at[gather.expert])
    for gather in soon:
        gather.start_across(pack_ref.at[gather.expert])
    xs_ref[ctx] = x_ref[...]
    dense_ref[dp] = dense_own_ref[...]
    full_ref[dp // 2, lax.rem(dp, 2)] = pack_ref[...]
    gr_ref[ctx] = cot_ref[...]

    segrow = seg_ref[...].astype(F32)
    for b in range(T // 128):
        segcol_ref[b * 128 : (b + 1) * 128, :] = column(segrow[:, b * 128 : (b + 1) * 128], 128, 0)
    chosen = []
    for k in range(LOCAL_EXPERTS):
        match = ids_ref[...] == ctx * LOCAL_EXPERTS + k
        chosen.append(jnp.sum(match.astype(F32), axis=0, keepdims=True))
        gate_ref[k : k + 1, :] = jnp.sum(jnp.where(match, gates_ref[...], 0.0), axis=0, keepdims=True)
    chosen = jnp.concatenate(chosen + [jnp.zeros((8 - LOCAL_EXPERTS, T), F32)], axis=0)
    earlier = lax.broadcasted_iota(jnp.int32, (128, 128), 0) < lax.broadcasted_iota(jnp.int32, (128, 128), 1)
    earlier = earlier.astype(F32).astype(BF16)
    for b in range(N_CTX):
        lanes = slice(b * 128, (b + 1) * 128)
        rank = dot(chosen[:, lanes].astype(BF16), earlier) + float(b % 2 * CAP)
        slot_ref[:, lanes] = jnp.where(chosen[:, lanes] > 0.5, rank, -1.0)

    rows_x.pass_on()
    place = lax.broadcasted_iota(jnp.int32, (SLOTS, BLOCK), 0).astype(F32)
    for pair in range(PAIRS):
        lanes = slice(pair * BLOCK, (pair + 1) * BLOCK)
        for k in range(LOCAL_EXPERTS):
            match = place == slot_ref[k : k + 1, lanes]
            pick_ref[pair, k * SLOTS : (k + 1) * SLOTS, :] = match.astype(F32).astype(BF16)
            gatecol_ref[k, pair * SLOTS : (pair + 1) * SLOTS, :] = jnp.sum(
                jnp.where(match, gate_ref[k : k + 1, lanes], 0.0), axis=1, keepdims=True
            )
    for gather in soon:
        gather.y_pass()
    rows_x.pass_far()
    def tables(rows):
        segcol = segcol_ref[rows, :]
        cfirst, sfirst = jnp.zeros((BLOCK, 128), F32), jnp.zeros((BLOCK, 128), F32)
        for d in range(5):
            cfirst = jnp.where(segcol == float(d), cfirst_ref[d : d + 1, :], cfirst)
            sfirst = jnp.where(segcol == float(d), sfirst_ref[d : d + 1, :], sfirst)
        ctab, stab = ctab_ref[rows, :], stab_ref[rows, :]
        sin = stab * cfirst - ctab * sfirst
        lane = lax.broadcasted_iota(jnp.int32, sin.shape, 1)
        return ctab * cfirst + stab * sfirst, jnp.where(lane % HD < HD // 2, -sin, sin)

    for made in dense:
        made.wait_recv()
    for k in range(N_DP):
        w_ref[k * 128 : (k + 1) * 128, :] = dense_ref[k, 0:128, :]
    gains = [
        jnp.concatenate([dense_ref[k, 128:144, 0:128] for k in range(N_DP)], axis=1).astype(F32)[n : n + 1]
        for n in range(2)
    ]
    rows_x.finish()

    @pl.when(dp != ctx)
    def _():
        swapped_in.wait_recv()

    rows_wout = RowGather(links, wouts_ref)
    rows_wout.start(wouts_ref.at[ctx])

    for r in range(T // BLOCK):
        rows = pl.ds(r * BLOCK, BLOCK)
        h = rms_norm(xs_ref[2 * r : 2 * r + 2].reshape(BLOCK, D).astype(F32), gains[0]).astype(BF16)
        h_ref[rows, :] = h
        qkv = dot(h, w_ref[...])
        cos, sin = tables(rows)
        query = qkv[:, :128]
        q_ref[rows, :] = (query * cos + swap_halves(query) * sin).astype(BF16)
        pair = qkv[:, 128:]
        turned = pair * cos + swap_halves(pair) * sin
        kv_ref[rows, :] = jnp.where(low_lanes(pair.shape), turned, pair).astype(BF16)

    rows_wout.pass_on()
    rows_gr = RowGather(links, gr_ref)
    rows_gr.start(cot_ref)
    low = low_lanes((BLOCK, 128))
    for r in range(T // BLOCK):
        rows = pl.ds(r * BLOCK, BLOCK)
        count = (r + 1) * BLOCK
        kv = kv_ref[0:count, :]
        query = q_ref[rows, :].astype(F32) * SCALE
        allowed = (segcol_ref[rows, :] == segrow[:, 0:count]) & (
            lax.broadcasted_iota(jnp.int32, (BLOCK, count), 0) + r * BLOCK
            >= lax.broadcasted_iota(jnp.int32, (BLOCK, count), 1)
        )
        outs = []
        for g in range(2):
            placed = query if g == 0 else pltpu.roll(query, HD, 1)
            placed = jnp.where(low, placed, 0.0).astype(BF16)
            scores = jnp.where(allowed, dot(placed, kv, ((1,), (1,))), NEGATIVE)
            largest = jnp.max(scores, axis=-1, keepdims=True)
            expon = jnp.exp(scores - largest)
            probs = (expon * (1.0 / jnp.sum(expon, axis=-1, keepdims=True))).astype(BF16)
            outs.append(dot(probs, kv))
        o_ref[2 * r : 2 * r + 2] = (
            jnp.where(low, pltpu.roll(outs[0], HD, 1), outs[1]).astype(BF16).reshape(2, 128, 128)
        )
        if r == 0:
            for gather in late:
                gather.pass_own()
            for gather in gathers[2:]:
                gather.start(pack_ref.at[gather.expert])
        if r == 1:
            rows_wout.pass_far()
            soon[0].pass_other()
            soon[0].pass_own()
        if r == 2:
            for gather in late:
                gather.y_start()
    outputs = exchange(links, o_ref, oall_ref, "ctx")
    rows_gr.pass_on()
    soon[1].pass_other()
    rows_wout.finish()
    for made in outputs:
        made.wait_recv()
    attended = jnp.concatenate([oall_ref[k] for k in range(N_CTX)], axis=1)
    x2 = x_ref[...].astype(F32) + dot(attended, wouts_ref[...].reshape(D, D))
    h2_ref[ctx] = rms_norm(x2, gains[1]).astype(BF16)
    rows_h2 = RowGather(links, h2_ref)
    rows_h2.start(h2_ref.at[ctx])
    for gather in late:
        gather.y_pass()
    rows_gr.pass_far()
    soon[1].pass_own()
    soon[2].pass_other()
    rows_h2.pass_on()
    soon[0].pass_last()
    soon[2].pass_own()
    rows_gr.finish()
    for pair in range(PAIRS):
        grads = dot(pick_ref[pair], gr_ref[2 * pair : 2 * pair + 2].reshape(BLOCK, D))
        for k in range(LOCAL_EXPERTS):
            here = slice(pair * SLOTS, (pair + 1) * SLOTS)
            dy_ref[k, here, :] = (grads[k * SLOTS : (k + 1) * SLOTS] * gatecol_ref[k, here, :]).astype(BF16)
    rows_h2.pass_far()
    soon[1].pass_last()
    rows_h2.finish()
    for pair in range(PAIRS):
        tokens = dot(pick_ref[pair], h2_ref[2 * pair : 2 * pair + 2].reshape(BLOCK, D)).astype(BF16)
        for k in range(LOCAL_EXPERTS):
            arrived_ref[k, pair * SLOTS : (pair + 1) * SLOTS, :] = tokens[k * SLOTS : (k + 1) * SLOTS]
    soon[2].pass_last()

    def down_of(e):
        return jnp.concatenate(
            [
                jnp.concatenate([full_ref[k // 2, k % 2, e, :, first : first + 128] for k in range(N_DP)], axis=1)
                for first in (2 * FH, 2 * FH + 128)
            ],
            axis=0,
        )

    def token_grads(e):
        gathers[e].finish()
        wgu = full_ref[:, :, e, :, 0 : 2 * FH].reshape(D, 2 * FH)
        gate_up = dot(arrived_ref[e], wgu)
        gate, up = gate_up[:, :FH], gate_up[:, FH:]
        sigma = jax.nn.sigmoid(gate)
        silu = gate * sigma
        hidden_ref[e] = (silu * up).astype(BF16)
        grad_hidden = dot(dy_ref[e], down_of(e), ((1,), (1,)))
        grad_gate = grad_hidden * up * (sigma * (1.0 + gate * (1.0 - sigma)))
        dgu_ref[e] = jnp.concatenate([grad_gate, grad_hidden * silu], axis=1).astype(BF16)
        back = dot(dgu_ref[e], wgu, ((1,), (1,))).astype(BF16)
        for pair in range(PAIRS):
            slots_ref[pair, e * SLOTS : (e + 1) * SLOTS, :] = back[pair * SLOTS : (pair + 1) * SLOTS]

    weights = [
        WeightSum(links, full_ref, relay_q_ref.at[1, e], gmid_q_ref.at[e], glast_q_ref.at[e], gother_q_ref.at[e], e, True)
        if e < LATE
        else WeightSum(
            links, full_ref, relay_p_ref.at[1, e - LATE], gmid_p_ref.at[e - LATE], glast_p_ref.at[e - LATE],
            gother_p_ref.at[e - LATE], e, False,
        )
        for e in range(LOCAL_EXPERTS)
    ]

    def weight_grads(e):
        hidden, dy = hidden_ref[e], dy_ref[e]
        out = (dot(hidden, down_of(e)) * gatecol_ref[e]).astype(BF16)
        grad_down = dot(hidden, dy, ((0,), (0,))).astype(BF16)
        dy_ref[e] = out
        links.settle(gathers[e].from_full())
        for k in range(N_DP):
            lanes = slice(k * 128, (k + 1) * 128)
            full_ref[k // 2, k % 2, e, :, 2 * FH : 2 * FH + 128] = grad_down[0:128, lanes]
            full_ref[k // 2, k % 2, e, :, 2 * FH + 128 :] = grad_down[128:256, lanes]
        grad_gateup = dot(arrived_ref[e], dgu_ref[e], ((0,), (0,))).astype(BF16)
        full_ref[:, :, e, :, 0 : 2 * FH] = grad_gateup.reshape(4, 2, 128, 2 * FH)
        weights[e].start()

    order = [1, 0, 2, 3]
    token_grads(order[0])
    token_grads(order[1])
    weight_grads(order[0])
    token_grads(order[2])
    weight_grads(order[1])
    token_grads(order[3])
    links.settle(rows_x.all())
    sum_dh2 = RowSum(links, xs_ref, near_ref.at[1], mid_ref.at[1], last_ref.at[1])
    for pair in range(PAIRS):
        rows_back = dot(pick_ref[pair], slots_ref[pair], ((0,), (0,))).astype(BF16)
        xs_ref[2 * pair : 2 * pair + 2] = rows_back.reshape(2, 128, D)
        sum_dh2.send(pair)
    weight_grads(order[2])
    sum_dh2.pair()
    weights[1].pass_on()
    weights[0].y_pass()
    weight_grads(order[3])
    sum_dh2.pass_on()
    links.settle(rows_gr.all())
    sum_y = RowSum(links, gr_ref, near_ref.at[2], mid_ref.at[2], last_ref.at[2])
    for pair in range(PAIRS):
        slot_rows = jnp.concatenate(
            [dy_ref[k, pair * SLOTS : (pair + 1) * SLOTS, :] for k in range(LOCAL_EXPERTS)], axis=0
        )
        rows_out = dot(pick_ref[pair], slot_rows, ((0,), (0,))).astype(BF16)
        gr_ref[2 * pair : 2 * pair + 2] = rows_out.reshape(2, 128, D)
        sum_y.send(pair)
    pairs_ref[0] = sum_dh2.finish().astype(BF16)
    swap = links.start(pairs_ref.at[0], pairs_ref.at[1], tensor=1 - tensor)
    sum_y.pair()
    weights[2].pass_on()
    inverse = lax.rsqrt(jnp.mean(x2 * x2, axis=-1, keepdims=True) + EPSILON)
    scaled = x2 * inverse
    swap.wait_recv()
    dh2 = pairs_ref[0].astype(F32) + pairs_ref[1].astype(F32)
    weighted = dh2 * gains[1]
    dx2 = cot_ref[...].astype(F32) + inverse * (
        weighted - scaled * jnp.mean(weighted * scaled, axis=-1, keepdims=True)
    )
    gradx_ref[...] = dx2
    da = dx2.astype(BF16)
    grad_heads = dot(da, wouts_ref[...].reshape(D, D), ((1,), (1,))).astype(BF16)
    for k in range(N_CTX):
        dosend_ref[k] = grad_heads[:, k * 128 : (k + 1) * 128]
    grad_outputs = exchange(links, dosend_ref, do_ref, "ctx")
    gain_two = jnp.sum(dh2 * scaled, axis=0, keepdims=True)
    gwsend_ref[:, 128:144, :] = jnp.zeros((N_DP, 16, 256), BF16)
    for k in range(N_DP):
        gwsend_ref[k, 128:144, 0:128] = jnp.broadcast_to(gain_two[:, k * 128 : (k + 1) * 128], (16, 128)).astype(BF16)
    sum_y.pass_on()
    links.settle(rows_h2.all())
    sum_out = RowSum(links, h2_ref, near_ref.at[0], mid_ref.at[0], last_ref.at[0])
    for k in range(N_CTX):
        h2_ref[k] = dot(oall_ref[k], da, ((0,), (0,))).astype(BF16)
    for z in range(4):
        sum_out.send(z)
    weights[3].pass_on()
    weights[0].y_add()
    weights[1].y_start()
    for made in grad_outputs:
        made.wait_recv()
    sum_out.pair()
    dkv_ref[...] = jnp.zeros_like(dkv_ref)
    links.settle(sum_dh2.sent)
    sum_dh = RowSum(links, xs_ref, near_ref.at[3], mid_ref.at[3], last_ref.at[3])
    for r in reversed(range(T // BLOCK)):
        rows = pl.ds(r * BLOCK, BLOCK)
        count = (r + 1) * BLOCK
        kv = kv_ref[0:count, :]
        query = q_ref[rows, :].astype(F32) * SCALE
        grad = do_ref[2 * r : 2 * r + 2].reshape(BLOCK, 128).astype(F32)
        allowed = (segcol_ref[0:count, :] == segrow[:, r * BLOCK : (r + 1) * BLOCK]) & (
            lax.broadcasted_iota(jnp.int32, (count, BLOCK), 1) + r * BLOCK
            >= lax.broadcasted_iota(jnp.int32, (count, BLOCK), 0)
        )
        grads = []
        for g in range(2):
            placed = query if g == 0 else pltpu.roll(query, HD, 1)
            placed = jnp.where(low, placed, 0.0).astype(BF16)
            placed_grad = grad if g == 1 else pltpu.roll(grad, HD, 1)
            placed_grad = jnp.where(low, 0.0, placed_grad).astype(BF16)
            scores = jnp.where(allowed, dot(kv, placed, ((1,), (1,))), NEGATIVE)
            largest = jnp.max(scores, axis=0, keepdims=True)
            expon = jnp.exp(scores - largest)
            probs = expon * (1.0 / jnp.sum(expon, axis=0, keepdims=True))
            grad_probs = dot(kv, placed_grad, ((1,), (1,)))
            delta = jnp.sum(grad_probs * probs, axis=0, keepdims=True)
            grad_scores = (probs * (grad_probs - delta)).astype(BF16)
            dkv_ref[0:count, :] += dot(grad_scores, placed) + dot(probs.astype(BF16), placed_grad)
            grads.append(dot(grad_scores, kv, ((0,), (0,))) * SCALE)
        grad_query = jnp.where(low, grads[0], pltpu.roll(grads[1], HD, 1))
        cos, sin = tables(rows)
        dqkv_ref[rows, 0:128] = (grad_query * cos - swap_halves(grad_query) * sin).astype(BF16)
        grad_pair = dkv_ref[rows, :]
        turned = grad_pair * cos - swap_halves(grad_pair) * sin
        dqkv_ref[rows, 128:256] = jnp.where(low, turned, grad_pair).astype(BF16)
        dh_part = dot(dqkv_ref[rows, :], w_ref[...], ((1,), (1,))).astype(BF16)
        xs_ref[2 * r : 2 * r + 2] = dh_part.reshape(2, 128, D)
        sum_dh.send(r)
        if r == 3:
            sum_out.pass_on()
            weights[1].y_pass()
        if r == 2:
            pairs_ref[2] = sum_y.finish().astype(BF16)
            swap_y = links.start(pairs_ref.at[2], pairs_ref.at[3], tensor=1 - tensor)
            weights[2].y_start()
        if r == 1:
            weights[2].y_pass()
            gosend_ref[...] = sum_out.finish().astype(BF16).reshape(N_CTX, 16, D)
            swapped = links.copy(gosend_ref, goswap_ref, dp=ctx, ctx=dp)

            @pl.when(dp != ctx)
            def _():
                swapped.start()

            @pl.when(dp == ctx)
            def _():
                goswap_ref[...] = gosend_ref[...]

    gw = dot(h_ref[...], dqkv_ref[...], ((0,), (0,)))
    gwsend_ref[:, 0:128, :] = gw.astype(BF16).reshape(N_DP, 128, 256)
    gwparts = exchange(links, gwsend_ref, gwparts_ref, "dp")
    sum_dh.pair()
    weights[3].y_start()
    weights[0].pass_on()

    @pl.when(dp != ctx)
    def _():
        swapped.wait_recv()

    goparts = exchange(links, goswap_ref, goparts_ref, "ctx")
    sum_dh.pass_on()
    weights[3].y_pass()
    for made in gwparts:
        made.wait_recv()
    mine = gwparts_ref[0].astype(F32)
    for k in range(1, N_DP):
        mine += gwparts_ref[k].astype(F32)
    for k in range(N_CTX):
        csend_ref[k, 0:16, :] = mine[k * 16 : (k + 1) * 16]
        csend_ref[k, 16:24, :] = mine[128:136]
    cparts = exchange(links, csend_ref, cparts_ref, "ctx")
    dh = sum_dh.finish()
    x_own = x_ref[...].astype(F32)
    inverse = lax.rsqrt(jnp.mean(x_own * x_own, axis=-1, keepdims=True) + EPSILON)
    scaled = x_own * inverse
    weighted = dh * gains[0]
    gradx_ref[...] += inverse * (weighted - scaled * jnp.mean(weighted * scaled, axis=-1, keepdims=True))
    for made in goparts:
        made.wait_recv()
    total_out = goparts_ref[0].astype(F32)
    for k in range(1, N_CTX):
        total_out += goparts_ref[k].astype(F32)
    gout_ref[...] = total_out
    swap_y.wait_recv()
    out_ref[...] = (x2 + (pairs_ref[2].astype(F32) + pairs_ref[3].astype(F32))).astype(BF16)
    for each in (weights[1], weights[2]):
        each.finish(outgu_ref, outd_ref)
    for made in cparts:
        made.wait_recv()
    gain_row = cparts_ref[0, 16:24, 0:128]
    for k in range(N_CTX):
        gq_ref[:, k * 128 : (k + 1) * 128] = cparts_ref[k, 0:16, 0:128]
        gkv_ref[:, k * 128 : (k + 1) * 128] = cparts_ref[k, 0:16, 128:256]
        if k > 0:
            gain_row += cparts_ref[k, 16:24, 0:128]
    own_rows = pl.ds(pl.multiple_of(ctx * 16, 16), 16)
    gain_one = jnp.sum(
        wq_ref[own_rows, :].astype(F32) * gq_ref[...] + wkv_ref[own_rows, :].astype(F32) * gkv_ref[...],
        axis=1,
        keepdims=True,
    ) / column(gains_own_ref[...].astype(F32)[0:1], 16, ctx * 16)
    gain_two = column(gain_row[0:1], 16, ctx * 16)
    lane = lax.broadcasted_iota(jnp.int32, (16, 128), 1)
    gains_ref[...] = jnp.where(lane == 0, gain_one, gain_two)
    for each in (weights[3], weights[0]):
        each.finish(outgu_ref, outd_ref)
    links.finish((swapped, swapped_in))

    @pl.when(dp != ctx)
    def _():
        swapped.wait_send()
        swapped_in.wait_send()


def layer(*args):
    shapes = [
        ((ROWS, D), BF16), ((ROWS, D), F32), ((16, D), F32), ((16, D), F32), ((16, 128), F32), ((16, D), F32),
        ((LOCAL_EXPERTS, 128, 2 * FH), F32), ((LOCAL_EXPERTS, FH, 128), F32),
    ]
    blocks = (N_CTX, ROWS, D)
    capacity = PAIRS * SLOTS
    scratch = [
        ((144, 256), BF16), ((N_DP, 144, 256), BF16), (blocks, BF16), ((LOCAL_EXPERTS, 128, WIDE), BF16),
        ((4, 2, LOCAL_EXPERTS, 128, WIDE), BF16), (blocks, BF16), (blocks, BF16), (blocks, BF16),
        ((4, 4, ROWS, D), BF16), ((4, 2, ROWS // 2, D), BF16), ((4, 2, ROWS, D), BF16), ((4, ROWS, D), BF16),
        ((D, 256), BF16), ((T, D), BF16), ((T, 128), BF16), ((T, 128), BF16), ((N_CTX, 128, 128), BF16),
        ((T, 1), F32), ((8, T), F32), ((LOCAL_EXPERTS, T), F32), ((LOCAL_EXPERTS, capacity, 1), F32),
        ((PAIRS, LOCAL_EXPERTS * SLOTS, BLOCK), BF16), ((LOCAL_EXPERTS, capacity, D), BF16),
        ((LOCAL_EXPERTS, capacity, D), BF16), ((LOCAL_EXPERTS, capacity, FH), BF16),
        ((LOCAL_EXPERTS, capacity, 2 * FH), BF16),
        ((PAIRS, LOCAL_EXPERTS * SLOTS, D), BF16),
        ((2, SOON, 2, 64, WIDE), BF16), ((2, LATE, 2, 4, 64, WIDE), BF16),
        ((SOON, 2, 2, 64, WIDE), BF16), ((LATE, 2, 64, WIDE), BF16),
        ((SOON, 2, 2, 128, WIDE), BF16), ((LATE, 2, 128, WIDE), BF16),
        ((SOON, 128, WIDE), BF16), ((LATE, 4, 128, WIDE), BF16), ((N_CTX, 128, 128), BF16), ((N_CTX, 128, 128), BF16),
        ((N_CTX, 128, 128), BF16),
        ((T, 128), F32), ((T, 256), BF16),
        ((N_CTX, 16, D), BF16), ((N_CTX, 16, D), BF16), ((N_CTX, 16, D), BF16), ((N_DP, 144, 256), BF16),
        ((N_DP, 144, 256), BF16), ((N_CTX, 24, 256), F32), ((N_CTX, 24, 256), F32),
    ]
    return pl.pallas_call(
        layer_kernel,
        out_shape=[jax.ShapeDtypeStruct(s, t) for s, t in shapes],
        in_specs=[pl.BlockSpec(memory_space=pltpu.VMEM)] * len(args),
        out_specs=[pl.BlockSpec(memory_space=pltpu.VMEM)] * len(shapes),
        scratch_shapes=[pltpu.VMEM(s, t) for s, t in scratch]
        + [pltpu.SemaphoreType.DMA((COPIES,)), pltpu.SemaphoreType.DMA((COPIES,))],
        compiler_params=pltpu.CompilerParams(
            vmem_limit_bytes=VMEM_LIMIT, collective_id=0, has_side_effects=True
        ),
        cost_estimate=pl.CostEstimate(flops=20_000_000_000, bytes_accessed=10_000_000, transcendentals=4_000_000),
        name="layer",
    )(*args)


def on_device(
    activations, cotangent, segment_ids, expert_ids, gate_weights, norm_gains, w_query, w_keyval, w_out, w_gateup, w_down
):
    frequency = np.exp(np.arange(HD // 2, dtype=np.float32) * np.float32(-2.0 * math.log(10000.0) / HD))
    frequency = np.tile(frequency.astype(np.float32), 4)[None, :]
    angles = (np.arange(T, dtype=np.float32)[:, None] * frequency).astype(np.float64)
    ctab, stab = np.cos(angles).astype(np.float32), np.sin(angles).astype(np.float32)
    documents = jnp.arange(8, dtype=jnp.int32)[:, None]
    first = jnp.sum((segment_ids < documents).astype(jnp.int32), axis=1, keepdims=True).astype(F32)
    out, grad_x, gq, gkv, gains, gout, grad_gateup, grad_down = layer(
        activations, cotangent, expert_ids[0].T, gate_weights[0].T, segment_ids, norm_gains[0], w_query[0], w_keyval[0],
        w_out[0], w_gateup[0].reshape(LOCAL_EXPERTS, 128, 2 * FH), w_down[0], jnp.asarray(ctab), jnp.asarray(stab),
        jnp.cos(first * frequency), jnp.sin(first * frequency),
    )
    return (
        out,
        grad_x,
        gains[:, 0:2].T[None],
        gq[None],
        gkv[None],
        gout[None],
        grad_gateup.reshape(1, LOCAL_EXPERTS, 128, 2, FH),
        grad_down[None],
    )


def solution(mesh):
    return jax.shard_map(
        on_device,
        mesh=mesh,
        in_specs=(
            P(("dp", "ctx"), None),
            P(("dp", "ctx"), None),
            P("dp", None),
            P(None, "dp", None),
            P(None, "dp", None),
            P(None, None, "dp"),
            P(None, "dp", None),
            P(None, "dp", None),
            P(None, "dp", None),
            P(None, "ctx", "dp", None, "tensor"),
            P(None, "ctx", "tensor", "dp"),
        ),
        out_specs=(
            P(("dp", "ctx"), None),
            P(("dp", "ctx"), None),
            P(None, None, ("dp", "ctx")),
            P(None, ("dp", "ctx"), None),
            P(None, ("dp", "ctx"), None),
            P(None, ("dp", "ctx"), None),
            P(None, "ctx", "dp", None, "tensor"),
            P(None, "ctx", "tensor", "dp"),
        ),
        check_vma=False,
    )
```
